32 devices in a mesh: ga: 2 (over y), aa: 4 (over x, core), ba: 4 (over z).
Axes of the slice: x: 2, y: 2, z: 4, core: 2. Of those that a mesh axis runs over, the one named last changes fastest.
Arguments:
- query: bfloat16 [2048, 5120], P(('ga', 'aa'), 'ba'), parts along dimension 0, may hold values from -64 to 64
- keys: bfloat16 [16384, 1024], P(('ga', 'aa'), 'ba'), parts along dimension 0, may hold values from -16 to 16
- values: bfloat16 [16384, 1024], P(('ga', 'aa'), 'ba'), parts along dimension 0, may hold values from -6 to 6
- cache_lengths: int32 [8], P(('ga', 'aa')), parts along dimension 0, may hold values from 256 to 2048, as said below
- residual: bfloat16 [2048, 5120], P(('ga', 'ba'), 'aa'), parts along dimension 0, may hold values from -16 to 16
- out_weight: bfloat16 [5120, 5120], P('ba', 'aa'), may hold values from -0.078125 to 0.078125
- norm_gain: float32 [5120], P('aa'), may hold values from 0.1 to 1.9
- router_weight: float32 [5120, 4], P('aa'), may hold values from -0.078125 to 0.078125
- expert_ids: int32 [2048], P(('ga', 'ba')), parts along dimension 0, may hold values from 0 to 3
- expert_slots: int32 [2048], P(('ga', 'ba')), parts along dimension 0, may hold values from -1 to 127, as said below
- expert_gate: bfloat16 [4, 5120, 4096], P('ba', None, 'aa'), may hold values from -0.078125 to 0.078125
- expert_up: bfloat16 [4, 5120, 4096], P('ba', None, 'aa'), may hold values from -0.078125 to 0.078125
- expert_down: bfloat16 [4, 4096, 5120], P('ba', 'aa'), may hold values from -0.25 to 0.25
Outputs:
- layer_out: bfloat16 [2048, 5120], P(('ga', 'ba'), 'aa'), parts along dimension 0
The draws below stay inside these ranges and needn't reach their ends.
There are 2 independent parts, one for each index of `ga`. The reference program is written for one: setup_inputs(seed, part) draws one part's arguments, and reference() takes and returns one part's arrays. A program takes and returns all parts, laid end to end along the dimension named above; an argument that names none is the same for every part. Nothing has to cross between parts.
Inputs may be any that keep to these rules, and one draw needn't show every extreme that they name: `cache_lengths`: some shard has 2048 valid positions in every draw. `expert_slots`: rows form aligned blocks of 256 rows (the rows of one index of ba). A row's slot is the number of earlier rows of its block with the same expert id, or -1 where that number is 128 or more. In every draw some expert has all 128 slots filled in every block.
All inputs are finite; a program needn't handle non-finite values.
Results may differ from the reference program's by a relative error of at most 0.019.
Values may be sent and summed in bfloat16 or wider, within the bound.
No kernel may reach another device: no remote copies, remote signals or barrier semaphores. Data moves between devices by JAX's collectives and lax.ppermute only.
A program may use at most 128 MiB of HBM per device.

```python
import jax
import jax.numpy as jnp
from jax import lax

D = 5120
H = 40
KVH = 8
HD = 128
FF = 4096
EXP_DEV = 1
Q = 1024
CTX_DEV = 2048
CTX = 8192
EXPERTS = 4
CAPS = 128


def draw_keys(key, part):
    base = jax.random.normal(jax.random.fold_in(key, 3), (CTX, KVH * HD), jnp.float32)
    return jnp.clip(base, -16.0, 16.0).astype(jnp.bfloat16)


def draw_query(key, part):
    base = 3.0 * jax.random.normal(jax.random.fold_in(key, 7), (Q, H * HD), jnp.float32)
    return jnp.clip(base, -64.0, 64.0).astype(jnp.bfloat16)


def draw_residual(key, part):
    columns = jnp.arange(D, dtype=jnp.float32) / D
    base = jax.random.normal(jax.random.fold_in(key, 11), (Q, D), jnp.float32) * (0.4 * 4.0 ** columns)[None, :]
    return jnp.clip(base, -16.0, 16.0).astype(jnp.bfloat16)


def draw_cache_lengths(key, part):
    shards = CTX // CTX_DEV
    lengths = jax.random.randint(jax.random.fold_in(key, 41), (shards,), CTX_DEV // 8, CTX_DEV + 1)
    full = jax.random.randint(jax.random.fold_in(key, 42), (), 0, shards)
    return lengths.at[full].set(CTX_DEV).astype(jnp.int32)


def routing(key):
    base = jax.random.fold_in(key, 29)
    blocks = EXPERTS // EXP_DEV
    rows = Q // blocks
    first = jax.random.randint(jax.random.fold_in(base, 1), (blocks, rows), 0, EXPERTS)
    second = jax.random.randint(jax.random.fold_in(base, 2), (blocks, rows), 0, EXPERTS)
    order = jax.random.permutation(jax.random.fold_in(base, 3), EXPERTS)
    ids = order[jnp.minimum(first, second)]
    scores = jax.random.randint(jax.random.fold_in(base, 4), (blocks, rows), 0, 1 << 20) * rows + jnp.arange(rows, dtype=jnp.int32)[None, :]
    ranks = jnp.argsort(jnp.argsort(scores, axis=1), axis=1)
    ids = jnp.where(ranks < CAPS, order[0], ids)
    onehot = (ids[..., None] == jnp.arange(EXPERTS, dtype=jnp.int32)[None, None, :]).astype(jnp.int32)
    earlier = jnp.sum((jnp.cumsum(onehot, axis=1) - onehot) * onehot, axis=-1)
    slots = jnp.where(earlier < CAPS, earlier, -1)
    return (ids.reshape(Q).astype(jnp.int32), slots.reshape(Q).astype(jnp.int32))


def draw_expert_ids(key, part):
    return routing(key)[0]


def draw_expert_slots(key, part):
    return routing(key)[1]


def block_scale(own_key, shape, pieces, low, high):
    level, own = 1.0, jax.random.fold_in(own_key, 6)
    for axis_at, parts in pieces:
        steps = jnp.exp(jax.random.uniform(jax.random.fold_in(own, axis_at), (parts,), jnp.float32, low / len(pieces), high / len(pieces)))
        level = level * jnp.repeat(steps, shape[axis_at] // parts).reshape([-1 if axis == axis_at else 1 for axis in range(len(shape))])
    return level


def bell_draw(stream_key, extent, width, bound, cuts=(), held_as=jnp.bfloat16):
    entries = jax.random.normal(stream_key, extent, jnp.float32) * width
    if len(cuts) > 0:
        entries = block_scale(stream_key, extent, cuts, -0.22, 0.18) * entries
    return jnp.clip(entries, min=-bound, max=bound).astype(held_as)


def setup_inputs(seed: int = 0, part: int = 0) -> dict:
    splits = jax.random.split(jax.random.key(seed), 14)
    part_splits = jax.random.split(jax.random.fold_in(splits[13], part), 14)
    return {
        "query": draw_query(jax.random.fold_in(jax.random.fold_in(splits[13], part), 71), part),
        "keys": draw_keys(jax.random.fold_in(jax.random.fold_in(splits[13], part), 71), part),
        "values": bell_draw(part_splits[2], (CTX, KVH * HD), 1.0, 6.0, ((0, 4), (1, 4))),
        "cache_lengths": draw_cache_lengths(jax.random.fold_in(jax.random.fold_in(splits[13], part), 71), part),
        "residual": draw_residual(jax.random.fold_in(jax.random.fold_in(splits[13], part), 71), part),
        "out_weight": bell_draw(splits[5], (H * HD, D), (H * HD) ** -0.5, 0.078125, ((0, 4), (1, 4))),
        "norm_gain": jnp.clip(1.0 + 0.18 * jax.random.normal(splits[6], (D,), jnp.float32), 0.1, 1.9),
        "router_weight": bell_draw(splits[7], (D, EXPERTS), D ** -0.5, 0.078125, ((0, 4),), jnp.float32),
        "expert_ids": draw_expert_ids(jax.random.fold_in(jax.random.fold_in(splits[13], part), 71), part),
        "expert_slots": draw_expert_slots(jax.random.fold_in(jax.random.fold_in(splits[13], part), 71), part),
        "expert_gate": bell_draw(splits[10], (EXPERTS, D, FF), D ** -0.5, 0.078125, ((0, 4), (2, 4))),
        "expert_up": bell_draw(splits[11], (EXPERTS, D, FF), D ** -0.5, 0.078125, ((0, 4), (2, 4))),
        "expert_down": bell_draw(splits[12], (EXPERTS, FF, D), (FF // 8) ** -0.5, 0.25, ((0, 4), (1, 4))),
    }


NEGATIVE = -1e+30
EPSILON = 1e-05

def reference(query, keys, values, cache_lengths, residual, out_weight, norm_gain, router_weight, expert_ids, expert_slots, expert_gate, expert_up, expert_down):
    group = H // KVH
    shards = CTX // CTX_DEV
    queries = query.astype(jnp.float32).reshape(Q, KVH, group, HD)

    def one_shard(index):
        start = (index * CTX_DEV).astype(jnp.int32)
        key_block = lax.dynamic_slice_in_dim(keys, start, CTX_DEV, 0).astype(jnp.float32).reshape(CTX_DEV, KVH, HD)
        value_block = lax.dynamic_slice_in_dim(values, start, CTX_DEV, 0).astype(jnp.float32).reshape(CTX_DEV, KVH, HD)
        scores = jnp.einsum('qkgd,tkd->kgqt', queries, key_block) * HD ** (-0.5)
        valid = jnp.arange(CTX_DEV, dtype=jnp.int32) < cache_lengths[index]
        scores = jnp.where(valid, scores, NEGATIVE)
        peak = lax.optimization_barrier(jnp.max(scores, axis=-1))
        probs = jnp.exp(scores - peak[..., None])
        total = lax.optimization_barrier(jnp.sum(probs, axis=-1))
        rounded = lax.optimization_barrier(probs.astype(jnp.bfloat16)).astype(jnp.float32)
        weighted = jnp.einsum('kgqt,tkd->kgqd', rounded, value_block)
        return (peak, total, weighted)
    peaks, totals, outputs = lax.map(one_shard, jnp.arange(shards, dtype=jnp.int32))
    top = lax.optimization_barrier(jnp.max(peaks, axis=0))
    factor = jnp.exp(peaks - top)
    numer = lax.optimization_barrier(jnp.sum(factor[..., None] * outputs, axis=0))
    denom = lax.optimization_barrier(jnp.sum(factor * totals, axis=0))
    attended = (numer / denom[..., None]).transpose(2, 0, 1, 3).reshape(Q, H * HD).astype(jnp.bfloat16)
    hidden = residual.astype(jnp.float32) + jnp.dot(attended, out_weight, preferred_element_type=jnp.float32)
    inverse = 1.0 / jnp.sqrt(lax.optimization_barrier(jnp.mean(hidden * hidden, axis=1)) + EPSILON)
    normed = hidden * inverse[:, None] * norm_gain
    logits = jnp.dot(normed, router_weight, precision=lax.Precision.HIGHEST)
    chosen = expert_ids[:, None] == jnp.arange(EXPERTS, dtype=jnp.int32)[None, :]
    gate = lax.optimization_barrier(jnp.sum(jnp.where(chosen, jax.nn.sigmoid(logits), 0.0), axis=1))
    expert_in = normed.astype(jnp.bfloat16)
    blocks = EXPERTS // EXP_DEV
    rows = Q // blocks
    combined = expert_ids * CAPS + expert_slots
    select = (combined[:, None] == jnp.arange(EXPERTS * CAPS, dtype=jnp.int32)[None, :]) & (expert_slots[:, None] >= 0)
    select = select.astype(jnp.float32).reshape(blocks, rows, EXPERTS, CAPS)
    buffer = jnp.einsum('brec,brd->ebcd', select, expert_in.astype(jnp.float32).reshape(blocks, rows, D))
    buffer = buffer.reshape(EXPERTS, blocks * CAPS, D).astype(jnp.bfloat16)

    def one_expert(operands):
        slots_in, gate_w, up_w, down_w = operands
        gate_part = jnp.dot(slots_in, gate_w, preferred_element_type=jnp.float32)
        up_part = jnp.dot(slots_in, up_w, preferred_element_type=jnp.float32)
        act = (jax.nn.silu(gate_part) * up_part).astype(jnp.bfloat16)
        return jnp.dot(act, down_w, preferred_element_type=jnp.float32).astype(jnp.bfloat16)
    outbuf = lax.map(one_expert, (buffer, expert_gate, expert_up, expert_down))
    outbuf = outbuf.reshape(EXPERTS, blocks, CAPS, D).astype(jnp.float32)
    back = jnp.einsum('brec,ebcd->brd', select, outbuf).reshape(Q, D)
    return (hidden + gate[:, None] * back).astype(jnp.bfloat16)
```

```python
import functools
import math

import jax
import jax.numpy as jnp
from jax import lax
from jax.experimental import pallas as pl
from jax.experimental.pallas import tpu as pltpu
from jax.sharding import PartitionSpec as P

HD = 128
KEY_BLOCK = 512
NEGATIVE = -1e30
EPSILON = 1e-05
SCALE = HD ** (-0.5)
SCALE_LOG2 = SCALE * math.log2(math.e)


def head_partials(rows, key_block, value_block, length):
    heads = rows.shape[1] // HD
    kv_heads = key_block.shape[1] // HD
    group = heads // kv_heads
    valid = lax.broadcasted_iota(jnp.int32, (1, key_block.shape[0]), 1) < length
    maxima = []
    totals = []
    outputs = []
    for head in range(heads):
        source = head // group
        q_head = rows[:, head * HD : (head + 1) * HD]
        k_head = key_block[:, source * HD : (source + 1) * HD]
        v_head = value_block[:, source * HD : (source + 1) * HD]
        scores = lax.dot_general(
            q_head, k_head, (((1,), (1,)), ((), ())), preferred_element_type=jnp.float32
        ) * SCALE
        scores = jnp.where(valid, scores, NEGATIVE)
        peak = jnp.max(scores, axis=1)
        probs = jnp.exp(scores - peak[:, None])
        maxima.append(peak)
        totals.append(jnp.sum(probs, axis=1))
        outputs.append(
            jnp.dot(probs.astype(jnp.bfloat16), v_head, preferred_element_type=jnp.float32)
        )
    return (jnp.stack(maxima, axis=1), jnp.stack(totals, axis=1), jnp.concatenate(outputs, axis=1))


def combine_partials(first, second):
    peak_one, total_one, out_one = first
    peak_two, total_two, out_two = second
    peak = jnp.maximum(peak_one, peak_two)
    scale_one = jnp.exp(peak_one - peak)
    scale_two = jnp.exp(peak_two - peak)
    outputs = out_one * jnp.repeat(scale_one, HD, axis=1) + out_two * jnp.repeat(
        scale_two, HD, axis=1
    )
    return (peak, total_one * scale_one + total_two * scale_two, outputs)


def plain_projection(query, keys, values, cache_lengths, out_weight):
    heads = query.shape[1] // HD
    own_rows = query.shape[0]
    context = keys.shape[0]
    start_state = (
        jnp.full((own_rows, heads), NEGATIVE, jnp.float32),
        jnp.zeros((own_rows, heads), jnp.float32),
        jnp.zeros((own_rows, heads * HD), jnp.float32),
    )
    key_piece = lax.all_gather(keys, "aa", axis=0, tiled=True)
    value_piece = lax.all_gather(values, "aa", axis=0, tiled=True)
    length_piece = lax.all_gather(cache_lengths, "aa", axis=0, tiled=True)

    def one_shard(index, carry):
        key_block = lax.dynamic_slice_in_dim(key_piece, index * context, context, 0)
        value_block = lax.dynamic_slice_in_dim(value_piece, index * context, context, 0)
        return combine_partials(
            carry, head_partials(query, key_block, value_block, length_piece[index])
        )

    peak, total, weighted = lax.fori_loop(0, length_piece.shape[0], one_shard, start_state)
    own = (weighted / jnp.repeat(total, HD, axis=1)).astype(jnp.bfloat16)
    attended = lax.all_gather(own, "aa", axis=0, tiled=True)
    return lax.psum_scatter(
        jnp.dot(attended, out_weight, preferred_element_type=jnp.float32).astype(jnp.bfloat16),
        "ba",
        scatter_dimension=0,
        tiled=True,
    ).astype(jnp.float32)


def attend_body(*refs, shards, units, resume, finish, block):
    lengths, q_ref = refs[0], refs[1]
    kv_refs = refs[2 : 2 + shards]
    at = 2 + shards
    if resume:
        peak_in, sums_in = refs[at : at + 2]
        at += 2
    if finish:
        out_ref, peak, sums = refs[at : at + 3]
    else:
        peak, sums = refs[at : at + 2]
    if resume:
        peak[...] = peak_in[...]
        sums[...] = sums_in[...]
    else:
        peak[...] = jnp.full(peak.shape, NEGATIVE, jnp.float32)
        sums[...] = jnp.zeros(sums.shape, jnp.float32)

    def one_block(kv_ref, base, length, tail):
        key = kv_ref[pl.ds(base, block), :HD]
        value = kv_ref[pl.ds(base, block), HD:]
        ones = jnp.ones((block, HD), jnp.bfloat16)
        if tail:
            valid = base + lax.broadcasted_iota(jnp.int32, (block, HD), 0) < length
            first = kv_ref[0:1, :HD].astype(jnp.float32)
            key = jnp.where(valid, key.astype(jnp.float32), first).astype(jnp.bfloat16)
            value = jnp.where(valid, value.astype(jnp.float32), 0.0).astype(jnp.bfloat16)
            ones = jnp.where(valid, 1.0, 0.0).astype(jnp.bfloat16)
        value = jnp.concatenate([value, ones], axis=1)

        def score(unit):
            return lax.dot_general(
                q_ref[:, unit * HD : (unit + 1) * HD],
                key,
                (((1,), (1,)), ((), ())),
                preferred_element_type=jnp.float32,
            )

        following = score(0)
        for unit in range(units):
            scores = following
            if unit + 1 < units:
                following = score(unit + 1)
            before = peak[unit]
            top = jnp.maximum(before, jnp.max(scores, axis=1, keepdims=True))
            peak[unit] = top
            probs = jnp.exp2(
                (scores - jnp.concatenate([top] * (block // HD), axis=1)) * SCALE_LOG2
            ).astype(jnp.bfloat16)
            fade = jnp.exp2((before - top) * SCALE_LOG2)
            sums[unit] = sums[unit] * jnp.concatenate([fade, fade], axis=1) + jnp.dot(
                probs, value, preferred_element_type=jnp.float32
            )

    for shard in range(shards):
        length = lengths[shard]
        whole = length // block
        kv_ref = kv_refs[shard]

        @pl.loop(0, whole)
        def _(step, kv_ref=kv_ref, length=length):
            one_block(kv_ref, pl.multiple_of(step * block, block), length, False)

        @pl.when(whole * block < length)
        def _(kv_ref=kv_ref, length=length, whole=whole):
            one_block(kv_ref, pl.multiple_of(whole * block, block), length, True)

    if finish:
        for unit in range(units):
            total = sums[unit]
            out_ref[:, unit * HD : (unit + 1) * HD] = (total[:, :HD] / total[:, HD:]).astype(
                jnp.bfloat16
            )


def attend(lengths, query, caches, state=None, finish=False):
    rows, width = query.shape
    units = width // HD
    shards = len(caches)
    peak = jax.ShapeDtypeStruct((units, rows, HD), jnp.float32)
    sums = jax.ShapeDtypeStruct((units, rows, 2 * HD), jnp.float32)
    vmem = pl.BlockSpec(memory_space=pltpu.VMEM)
    operands = [query, *caches]
    if state is not None:
        operands += list(state)
    if finish:
        out_shape = jax.ShapeDtypeStruct(query.shape, jnp.bfloat16)
        out_specs = vmem
        scratch = [pltpu.VMEM(peak.shape, peak.dtype), pltpu.VMEM(sums.shape, sums.dtype)]
    else:
        out_shape = (peak, sums)
        out_specs = (vmem, vmem)
        scratch = []
    positions = sum(cache.shape[0] for cache in caches)
    return pl.pallas_call(
        functools.partial(
            attend_body,
            shards=shards,
            units=units,
            resume=state is not None,
            finish=finish,
            block=KEY_BLOCK,
        ),
        out_shape=out_shape,
        in_specs=[pl.BlockSpec(memory_space=pltpu.SMEM)] + [vmem] * len(operands),
        out_specs=out_specs,
        scratch_shapes=scratch,
        compiler_params=pltpu.CompilerParams(vmem_limit_bytes=40 * 1024 * 1024),
        cost_estimate=pl.CostEstimate(
            flops=8 * rows * width * positions,
            bytes_accessed=2 * rows * width + 4 * positions * HD,
            transcendentals=rows * units * positions,
        ),
    )(lengths, *operands)


def swap_pairs(size, mask):
    return [(index, index ^ mask) for index in range(size)]


def split_projection(query, keys, values, cache_lengths, out_weight):
    size = lax.axis_size("aa")
    index = lax.axis_index("aa")
    side = index // 2
    over = functools.partial(lax.ppermute, axis_name="aa", perm=swap_pairs(size, 2))
    core = functools.partial(lax.ppermute, axis_name="aa", perm=swap_pairs(size, 1))
    half = query.shape[1] // 2

    def mine(array, which):
        width = array.shape[1] // 2
        return lax.dynamic_slice_in_dim(array, which * width, width, 1)

    far_query = over(mine(query, 1 - side))
    far_cache = over(jnp.concatenate([mine(keys, 1 - side), mine(values, 1 - side)], axis=1))
    own_query = mine(query, side)
    own_cache = jnp.concatenate([mine(keys, side), mine(values, side)], axis=1)
    near_cache = core(own_cache)
    corner_cache = core(far_cache)
    near_length = core(cache_lengths)
    far_length = over(cache_lengths)
    corner_length = core(far_length)

    close = jnp.concatenate([cache_lengths, near_length])
    own_state = attend(close, own_query, [own_cache, near_cache])
    far_state = attend(close, far_query, [own_cache, near_cache])
    own_state = attend(far_length, own_query, [far_cache], own_state)
    far_state = attend(far_length, far_query, [far_cache], far_state)
    own_rows = attend(corner_length, own_query, [corner_cache], own_state, True)
    far_rows = attend(corner_length, far_query, [corner_cache], far_state, True)

    own_other = over(far_rows)
    far_other = over(own_rows)
    first = jnp.stack([own_rows, far_rows, core(own_rows), core(far_rows)])
    second = jnp.stack([own_other, far_other, core(own_other), core(far_other)])
    first_weight = lax.dynamic_slice_in_dim(out_weight, side * half, half, 0)
    second_weight = lax.dynamic_slice_in_dim(out_weight, (1 - side) * half, half, 0)

    place = lax.axis_index("ba")
    order = jnp.array([[3, 2, 1, 0], [3, 2, 0, 1], [0, 1, 3, 2], [0, 1, 2, 3]], jnp.int32)[place]
    slot_of = jnp.array([0, 2, 1, 3], jnp.int32)

    def product(step):
        slot = slot_of[index ^ order[step]]
        left = lax.dynamic_index_in_dim(first, slot, 0, False)
        right = lax.dynamic_index_in_dim(second, slot, 0, False)
        return jnp.dot(left, first_weight, preferred_element_type=jnp.float32) + jnp.dot(
            right, second_weight, preferred_element_type=jnp.float32
        )

    def add(one, two):
        return (one.astype(jnp.float32) + two.astype(jnp.float32)).astype(jnp.bfloat16)

    right = functools.partial(lax.ppermute, axis_name="ba")
    left = functools.partial(lax.ppermute, axis_name="ba")
    one = product(0).astype(jnp.bfloat16)
    up = right(one, perm=[(0, 1)])
    down = left(one, perm=[(3, 2)])
    two = product(1).astype(jnp.bfloat16)
    up = right(add(jnp.where(place == 0, two, one), up), perm=[(0, 1), (1, 2)])
    down = left(add(jnp.where(place == 3, two, one), down), perm=[(3, 2), (2, 1)])
    three = product(2).astype(jnp.bfloat16)
    up = right(add(jnp.where(place == 1, two, three), up), perm=[(0, 1), (1, 2), (2, 3)])
    down = left(add(jnp.where(place == 2, two, three), down), perm=[(3, 2), (2, 1), (1, 0)])
    return product(3) + up.astype(jnp.float32) + down.astype(jnp.float32)


def on_device(
    query,
    keys,
    values,
    cache_lengths,
    residual,
    out_weight,
    norm_gain,
    router_weight,
    expert_ids,
    expert_slots,
    expert_gate,
    expert_up,
    expert_down,
):
    split = (
        lax.axis_size("aa") == 4
        and lax.axis_size("ba") == 4
        and keys.shape[1] == 2 * HD
        and keys.shape[0] % KEY_BLOCK == 0
        and query.shape[0] == residual.shape[0]
    )
    project = split_projection if split else plain_projection
    hidden = residual.astype(jnp.float32) + project(
        query, keys, values, cache_lengths, out_weight
    )
    width = hidden.shape[1] * lax.axis_size("aa")
    experts = router_weight.shape[1]
    gained = hidden * norm_gain
    squares = jnp.sum(hidden * hidden, axis=1, keepdims=True)
    raw = jnp.dot(gained, router_weight, precision=lax.Precision.HIGHEST)
    sums = lax.psum(jnp.concatenate([squares, raw], axis=1), "aa")
    inverse = 1.0 / jnp.sqrt(sums[:, :1] / width + EPSILON)
    logits = sums[:, 1:] * inverse
    normed = gained * inverse
    chosen = expert_ids[:, None] == lax.broadcasted_iota(jnp.int32, (1, experts), 1)
    gate = jnp.sum(jnp.where(chosen, jax.nn.sigmoid(logits), 0.0), axis=1)
    expert_in = normed.astype(jnp.bfloat16)
    slot_count = 2 * query.shape[0] * lax.axis_size("aa") // (lax.axis_size("ba") * experts)
    combined = expert_ids * slot_count + expert_slots
    placing = (
        combined[:, None] == lax.broadcasted_iota(jnp.int32, (1, experts * slot_count), 1)
    ) & (expert_slots[:, None] >= 0)
    placing = placing.astype(jnp.bfloat16)
    packed = lax.dot_general(
        placing, expert_in, (((0,), (0,)), ((), ())), preferred_element_type=jnp.float32
    ).astype(jnp.bfloat16)
    arrived = lax.all_to_all(packed, "ba", split_axis=0, concat_axis=0, tiled=True)
    gate_w = expert_gate[0]
    up_w = expert_up[0]
    down_w = expert_down[0]
    piece = lax.all_gather(arrived, "aa", axis=1, tiled=True)
    gate_part = jnp.dot(piece, gate_w, preferred_element_type=jnp.float32)
    up_part = jnp.dot(piece, up_w, preferred_element_type=jnp.float32)
    act = (jax.nn.silu(gate_part) * up_part).astype(jnp.bfloat16)
    expert_out = lax.psum_scatter(
        lax.dot_general(
            down_w, act, (((0,), (1,)), ((), ())), preferred_element_type=jnp.float32
        ).astype(jnp.bfloat16),
        "aa",
        scatter_dimension=0,
        tiled=True,
    )
    returned = lax.all_to_all(expert_out, "ba", split_axis=1, concat_axis=1, tiled=True)
    from_experts = lax.dot_general(
        placing, returned, (((1,), (1,)), ((), ())), preferred_element_type=jnp.float32
    )
    return (hidden + gate[:, None] * from_experts).astype(jnp.bfloat16)


def solution(mesh):
    return jax.shard_map(
        on_device,
        mesh=mesh,
        in_specs=(
            P(("ga", "aa"), "ba"),
            P(("ga", "aa"), "ba"),
            P(("ga", "aa"), "ba"),
            P(("ga", "aa")),
            P(("ga", "ba"), "aa"),
            P("ba", "aa"),
            P("aa"),
            P("aa", None),
            P(("ga", "ba")),
            P(("ga", "ba")),
            P("ba", None, "aa"),
            P("ba", None, "aa"),
            P("ba", "aa", None),
        ),
        out_specs=P(("ga", "ba"), "aa"),
        check_vma=False,
    )
```

```python
import functools
import math

import jax
import jax.numpy as jnp
from jax import lax
from jax.experimental import pallas as pl
from jax.experimental.pallas import tpu as pltpu
from jax.sharding import PartitionSpec as P

HD = 128
KEY_BLOCK = 1024
STEP = 256
MARKS = 32
SMALL_VMEM = 16 * 1024 * 1024
EXPERT_VMEM = 20 * 1024 * 1024
NEGATIVE = -1e30
EPSILON = 1e-05
SCALE = HD ** (-0.5)
SCALE_LOG2 = SCALE * math.log2(math.e)


def head_partials(rows, key_block, value_block, length):
    heads = rows.shape[1] // HD
    kv_heads = key_block.shape[1] // HD
    group = heads // kv_heads
    valid = lax.broadcasted_iota(jnp.int32, (1, key_block.shape[0]), 1) < length
    maxima = []
    totals = []
    outputs = []
    for head in range(heads):
        source = head // group
        q_head = rows[:, head * HD : (head + 1) * HD]
        k_head = key_block[:, source * HD : (source + 1) * HD]
        v_head = value_block[:, source * HD : (source + 1) * HD]
        scores = lax.dot_general(
            q_head, k_head, (((1,), (1,)), ((), ())), preferred_element_type=jnp.float32
        ) * SCALE
        scores = jnp.where(valid, scores, NEGATIVE)
        peak = jnp.max(scores, axis=1)
        probs = jnp.exp(scores - peak[:, None])
        maxima.append(peak)
        totals.append(jnp.sum(probs, axis=1))
        outputs.append(
            jnp.dot(probs.astype(jnp.bfloat16), v_head, preferred_element_type=jnp.float32)
        )
    return (jnp.stack(maxima, axis=1), jnp.stack(totals, axis=1), jnp.concatenate(outputs, axis=1))


def combine_partials(first, second):
    peak_one, total_one, out_one = first
    peak_two, total_two, out_two = second
    peak = jnp.maximum(peak_one, peak_two)
    scale_one = jnp.exp(peak_one - peak)
    scale_two = jnp.exp(peak_two - peak)
    outputs = out_one * jnp.repeat(scale_one, HD, axis=1) + out_two * jnp.repeat(
        scale_two, HD, axis=1
    )
    return (peak, total_one * scale_one + total_two * scale_two, outputs)


def plain_projection(query, keys, values, cache_lengths, out_weight):
    heads = query.shape[1] // HD
    own_rows = query.shape[0]
    context = keys.shape[0]
    start_state = (
        jnp.full((own_rows, heads), NEGATIVE, jnp.float32),
        jnp.zeros((own_rows, heads), jnp.float32),
        jnp.zeros((own_rows, heads * HD), jnp.float32),
    )
    key_piece = lax.all_gather(keys, "aa", axis=0, tiled=True)
    value_piece = lax.all_gather(values, "aa", axis=0, tiled=True)
    length_piece = lax.all_gather(cache_lengths, "aa", axis=0, tiled=True)

    def one_shard(index, carry):
        key_block = lax.dynamic_slice_in_dim(key_piece, index * context, context, 0)
        value_block = lax.dynamic_slice_in_dim(value_piece, index * context, context, 0)
        return combine_partials(
            carry, head_partials(query, key_block, value_block, length_piece[index])
        )

    peak, total, weighted = lax.fori_loop(0, length_piece.shape[0], one_shard, start_state)
    own = (weighted / jnp.repeat(total, HD, axis=1)).astype(jnp.bfloat16)
    attended = lax.all_gather(own, "aa", axis=0, tiled=True)
    return lax.psum_scatter(
        jnp.dot(attended, out_weight, preferred_element_type=jnp.float32).astype(jnp.bfloat16),
        "ba",
        scatter_dimension=0,
        tiled=True,
    ).astype(jnp.float32)


def prepare_body(scalars, q_ref, k_ref, v_ref, own_query, far_query, own_cache, far_cache):
    side, length = scalars[0], scalars[1]
    context = k_ref.shape[0]
    half = q_ref.shape[1] // 2
    marks = far_cache.shape[0] - context
    high = jnp.full((marks // 2, 2 * HD), length // 256, jnp.int32).astype(jnp.float32)
    low = jnp.full((marks // 2, 2 * HD), lax.rem(length, 256), jnp.int32).astype(jnp.float32)
    for query_out, cache_out, which in (
        (own_query, own_cache, side),
        (far_query, far_cache, 1 - side),
    ):
        query_out[...] = q_ref[:, pl.ds(pl.multiple_of(which * half, HD), half)]
        column = pl.ds(pl.multiple_of(which * HD, HD), HD)
        cache_out[:context, :HD] = k_ref[:, column]
        cache_out[:context, HD:] = v_ref[:, column]
        cache_out[context : context + marks // 2, :] = high.astype(jnp.bfloat16)
        cache_out[context + marks // 2 :, :] = low.astype(jnp.bfloat16)


def prepare(side, cache_lengths, query, keys, values):
    scalars = jnp.concatenate([side[None].astype(jnp.int32), cache_lengths])
    vmem = pl.BlockSpec(memory_space=pltpu.VMEM)
    half = jax.ShapeDtypeStruct((query.shape[0], query.shape[1] // 2), jnp.bfloat16)
    cache = jax.ShapeDtypeStruct((keys.shape[0] + MARKS, 2 * HD), jnp.bfloat16)
    return pl.pallas_call(
        prepare_body,
        out_shape=(half, half, cache, cache),
        in_specs=[pl.BlockSpec(memory_space=pltpu.SMEM), vmem, vmem, vmem],
        out_specs=(vmem, vmem, vmem, vmem),
        compiler_params=pltpu.CompilerParams(vmem_limit_bytes=SMALL_VMEM),
    )(scalars, query, keys, values)


def attend_body(*refs, shards, units, resume, finish, block):
    q_ref = refs[0]
    kv_refs = refs[1 : 1 + shards]
    at = 1 + shards
    if resume:
        peak_in, sums_in = refs[at : at + 2]
        at += 2
    if finish:
        out_ref, peak, sums = refs[at : at + 3]
    else:
        peak, sums = refs[at : at + 2]
    if resume:
        peak[...] = peak_in[...]
        sums[...] = sums_in[...]
    else:
        peak[...] = jnp.full(peak.shape, NEGATIVE, jnp.float32)
        sums[...] = jnp.zeros(sums.shape, jnp.float32)

    def one_block(kv_ref, base, length, high, tail):
        key = kv_ref[pl.ds(base, high), :HD]
        value = kv_ref[pl.ds(base, high), HD:]
        ones = jnp.ones((high, HD), jnp.bfloat16)
        if tail:
            valid = base + lax.broadcasted_iota(jnp.int32, (high, HD), 0) < length
            first = kv_ref[0:16, :HD].astype(jnp.float32)[0:1]
            key = jnp.where(valid, key.astype(jnp.float32), first).astype(jnp.bfloat16)
            value = jnp.where(valid, value.astype(jnp.float32), 0.0).astype(jnp.bfloat16)
            ones = jnp.where(valid, 1.0, 0.0).astype(jnp.bfloat16)
        value = jnp.concatenate([value, ones], axis=1)

        def score(unit):
            return lax.dot_general(
                q_ref[:, unit * HD : (unit + 1) * HD],
                key,
                (((1,), (1,)), ((), ())),
                preferred_element_type=jnp.float32,
            )

        following = score(0)
        for unit in range(units):
            scores = following
            if unit + 1 < units:
                following = score(unit + 1)
            before = peak[unit]
            top = jnp.maximum(before, jnp.max(scores, axis=1, keepdims=True))
            peak[unit] = top
            probs = jnp.exp2(
                (scores - jnp.concatenate([top] * (high // HD), axis=1)) * SCALE_LOG2
            ).astype(jnp.bfloat16)
            fade = jnp.exp2((before - top) * SCALE_LOG2)
            sums[unit] = sums[unit] * jnp.concatenate([fade, fade], axis=1) + jnp.dot(
                probs, value, preferred_element_type=jnp.float32
            )

    for shard in range(shards):
        kv_ref = kv_refs[shard]
        context = kv_ref.shape[0] - MARKS
        marks = jnp.max(
            kv_ref[context : context + MARKS, :HD].astype(jnp.float32).reshape(2, MARKS // 2, HD),
            axis=1,
        ).astype(jnp.int32)
        length = jnp.max(marks[0:1]) * 256 + jnp.max(marks[1:2])
        whole = length // block
        left = length - whole * block

        @pl.loop(0, whole)
        def _(step, kv_ref=kv_ref, length=length):
            one_block(kv_ref, pl.multiple_of(step * block, block), length, block, False)

        for high in range(STEP, block + 1, STEP):

            @pl.when(jnp.logical_and(left > high - STEP, left <= high))
            def _(kv_ref=kv_ref, length=length, whole=whole, high=high):
                one_block(kv_ref, pl.multiple_of(whole * block, block), length, high, True)

    if finish:
        for unit in range(units):
            total = sums[unit]
            out_ref[:, unit * HD : (unit + 1) * HD] = (total[:, :HD] / total[:, HD:]).astype(
                jnp.bfloat16
            )


def attend(query, caches, state=None, finish=False):
    rows, width = query.shape
    units = width // HD
    shards = len(caches)
    peak = jax.ShapeDtypeStruct((units, rows, HD), jnp.float32)
    sums = jax.ShapeDtypeStruct((units, rows, 2 * HD), jnp.float32)
    vmem = pl.BlockSpec(memory_space=pltpu.VMEM)
    operands = [query, *caches]
    if state is not None:
        operands += list(state)
    if finish:
        out_shape = jax.ShapeDtypeStruct(query.shape, jnp.bfloat16)
        out_specs = vmem
        scratch = [pltpu.VMEM(peak.shape, peak.dtype), pltpu.VMEM(sums.shape, sums.dtype)]
    else:
        out_shape = (peak, sums)
        out_specs = (vmem, vmem)
        scratch = []
    positions = sum(cache.shape[0] for cache in caches)
    return pl.pallas_call(
        functools.partial(
            attend_body,
            shards=shards,
            units=units,
            resume=state is not None,
            finish=finish,
            block=KEY_BLOCK,
        ),
        out_shape=out_shape,
        in_specs=[vmem] * len(operands),
        out_specs=out_specs,
        scratch_shapes=scratch,
        compiler_params=pltpu.CompilerParams(vmem_limit_bytes=SMALL_VMEM),
        cost_estimate=pl.CostEstimate(
            flops=8 * rows * width * positions,
            bytes_accessed=2 * rows * width + 4 * positions * HD,
            transcendentals=rows * units * positions,
        ),
    )(*operands)


def swap_pairs(size, mask):
    return [(index, index ^ mask) for index in range(size)]


def add(one, two):
    return (one.astype(jnp.float32) + two.astype(jnp.float32)).astype(jnp.bfloat16)


def split_projection(query, keys, values, cache_lengths, out_weight):
    size = lax.axis_size("aa")
    index = lax.axis_index("aa")
    side = index // 2
    over = functools.partial(lax.ppermute, axis_name="aa", perm=swap_pairs(size, 2))
    core = functools.partial(lax.ppermute, axis_name="aa", perm=swap_pairs(size, 1))
    half = query.shape[1] // 2

    own_query, away_query, own_cache, away_cache = prepare(
        side, cache_lengths, query, keys, values
    )
    far_query = over(away_query)
    far_cache = over(away_cache)
    near_cache = core(own_cache)
    own_state = attend(own_query, [own_cache, near_cache])
    far_state = attend(far_query, [own_cache, near_cache])
    far_cache, own_state, far_state = lax.optimization_barrier((far_cache, own_state, far_state))
    corner_cache = core(far_cache)
    own_state = attend(own_query, [far_cache], own_state)
    far_state = attend(far_query, [far_cache], far_state)
    own_rows = attend(own_query, [corner_cache], own_state, True)
    far_rows = attend(far_query, [corner_cache], far_state, True)

    own_other = over(far_rows)
    far_other = over(own_rows)
    first = jnp.stack([own_rows, far_rows, core(own_rows), core(far_rows)])
    second = jnp.stack([own_other, far_other, core(own_other), core(far_other)])
    first_weight = lax.dynamic_slice_in_dim(out_weight, side * half, half, 0)
    second_weight = lax.dynamic_slice_in_dim(out_weight, (1 - side) * half, half, 0)

    place = lax.axis_index("ba")
    order = jnp.array([[3, 2, 1, 0], [3, 2, 0, 1], [0, 1, 3, 2], [0, 1, 2, 3]], jnp.int32)[place]
    slot_of = jnp.array([0, 2, 1, 3], jnp.int32)
    columns = out_weight.shape[1]
    cut = columns // 2 if columns % (2 * HD) == 0 else columns

    def product(step, begin):
        slot = slot_of[index ^ order[step]]
        left = lax.dynamic_index_in_dim(first, slot, 0, False)
        right = lax.dynamic_index_in_dim(second, slot, 0, False)
        return jnp.dot(
            left, first_weight[:, begin : begin + cut], preferred_element_type=jnp.float32
        ) + jnp.dot(
            right, second_weight[:, begin : begin + cut], preferred_element_type=jnp.float32
        )

    send = functools.partial(lax.ppermute, axis_name="ba")
    starts = range(0, columns, cut)
    one = [product(0, begin).astype(jnp.bfloat16) for begin in starts]
    up = [send(part, perm=[(0, 1)]) for part in one]
    down = [send(part, perm=[(3, 2)]) for part in one]
    two = [product(1, begin).astype(jnp.bfloat16) for begin in starts]
    for at in range(len(one)):
        up[at] = send(
            add(jnp.where(place == 0, two[at], one[at]), up[at]), perm=[(0, 1), (1, 2)]
        )
        down[at] = send(
            add(jnp.where(place == 3, two[at], one[at]), down[at]), perm=[(3, 2), (2, 1)]
        )
    three = [product(2, begin).astype(jnp.bfloat16) for begin in starts]
    for at in range(len(one)):
        up[at] = send(
            add(jnp.where(place == 1, two[at], three[at]), up[at]),
            perm=[(0, 1), (1, 2), (2, 3)],
        )
        down[at] = send(
            add(jnp.where(place == 2, two[at], three[at]), down[at]),
            perm=[(3, 2), (2, 1), (1, 0)],
        )
    return jnp.concatenate(
        [
            product(3, begin) + up[at].astype(jnp.float32) + down[at].astype(jnp.float32)
            for at, begin in enumerate(starts)
        ],
        axis=1,
    )


def expert_body(quarter, *refs, blocks, tile):
    piece_refs = refs[: 4 * blocks]
    scale_refs = refs[4 * blocks : 5 * blocks]
    gate_ref, up_ref, down_ref, out_ref, act = refs[5 * blocks :]
    rows, width = piece_refs[0].shape
    hidden_units = gate_ref.shape[2]
    diagonal = lax.broadcasted_iota(jnp.int32, (rows, rows), 0) == lax.broadcasted_iota(
        jnp.int32, (rows, rows), 1
    )
    scale = jnp.concatenate(
        [
            jnp.sum(jnp.where(diagonal, scale_ref[...], 0.0), axis=1, keepdims=True)
            for scale_ref in scale_refs
        ],
        axis=0,
    )
    for begin in range(0, hidden_units, tile):
        columns = slice(begin, begin + tile)
        gate_sum = up_sum = 0.0
        for piece in range(4):
            operand = jnp.concatenate(
                [piece_refs[4 * block + piece][...] for block in range(blocks)], axis=0
            )
            at = pl.ds(pl.multiple_of(quarter[piece] * width, width), width)
            gate_sum += jnp.dot(operand, gate_ref[0, at, columns], preferred_element_type=jnp.float32)
            up_sum += jnp.dot(operand, up_ref[0, at, columns], preferred_element_type=jnp.float32)
        gate_sum = gate_sum * scale
        act[:, columns] = (
            gate_sum / (1.0 + jnp.exp(-gate_sum)) * (up_sum * scale)
        ).astype(jnp.bfloat16)
    for piece in range(4):
        for begin in range(0, width, tile):
            at = pl.ds(pl.multiple_of(quarter[piece] * width + begin, HD), tile)
            out_ref[piece, :, begin : begin + tile] = jnp.dot(
                act[...], down_ref[0, :, at], preferred_element_type=jnp.float32
            ).astype(jnp.bfloat16)


def expert_call(quarter, pieces, scales, gate_w, up_w, down_w):
    blocks = len(pieces)
    rows, width = pieces[0][0].shape
    hidden_units = gate_w.shape[2]
    high = blocks * rows
    vmem = pl.BlockSpec(memory_space=pltpu.VMEM)
    flat = [piece for block in pieces for piece in block] + list(scales)
    return pl.pallas_call(
        functools.partial(expert_body, blocks=blocks, tile=2 * HD),
        in_specs=[pl.BlockSpec(memory_space=pltpu.SMEM)] + [vmem] * (len(flat) + 3),
        out_specs=vmem,
        out_shape=jax.ShapeDtypeStruct((4, high, width), jnp.bfloat16),
        scratch_shapes=[pltpu.VMEM((high, hidden_units), jnp.bfloat16)],
        compiler_params=pltpu.CompilerParams(vmem_limit_bytes=EXPERT_VMEM),
        cost_estimate=pl.CostEstimate(
            flops=6 * high * 4 * width * hidden_units,
            bytes_accessed=24 * width * hidden_units,
            transcendentals=high * hidden_units,
        ),
    )(quarter, *flat, gate_w, up_w, down_w)


def routed_experts(gained, inverse, expert_ids, expert_slots, slot_count, gate_w, up_w, down_w):
    size = lax.axis_size("aa")
    index = lax.axis_index("aa")
    depth = lax.axis_size("ba")
    place = lax.axis_index("ba")
    over = functools.partial(lax.ppermute, axis_name="aa", perm=swap_pairs(size, 2))
    core = functools.partial(lax.ppermute, axis_name="aa", perm=swap_pairs(size, 1))

    def shift(array, by):
        return lax.ppermute(
            array, "ba", perm=[(at, (at + by) % depth) for at in range(depth)]
        )

    ahead = lax.rem(expert_ids - place + depth, depth)
    combined = ahead * slot_count + expert_slots
    chosen = (
        combined[:, None] == lax.broadcasted_iota(jnp.int32, (1, depth * slot_count), 1)
    ) & (expert_slots[:, None] >= 0)
    placing = chosen.astype(jnp.bfloat16)
    rows = gained.astype(jnp.bfloat16)
    slots = [slice(at * slot_count, (at + 1) * slot_count) for at in range(depth)]
    parts = [
        lax.dot_general(
            placing[:, slots[at]], rows, (((0,), (0,)), ((), ())), preferred_element_type=jnp.float32
        ).astype(jnp.bfloat16)
        for at in range(depth)
    ]

    def widen(block):
        far = over(block)
        both = core(jnp.stack([block, far]))
        return [block, far, both[0], both[1]]

    arrived = [parts[0], shift(parts[1], 1), None, shift(parts[3], 3)]
    factor = jnp.sum(jnp.where(chosen, inverse, 0.0), axis=0, keepdims=True)
    factors = [factor[:, slots[at]] for at in range(depth)]
    factors[1:] = [shift(factors[at], at) for at in range(1, depth)]
    last, factor = lax.optimization_barrier((parts[2], factor))
    arrived[2] = shift(last, 2)
    quarter = jnp.stack([index, index ^ 2, index ^ 1, index ^ 3]).astype(jnp.int32)

    def narrow(share):
        return add(share[:2], core(share[2:]))

    weights = (gate_w, up_w, down_w)
    one = expert_call(quarter, [widen(arrived[0]), widen(arrived[1])], factors[:2], *weights)
    one = narrow(one)
    later = [widen(arrived[3]), widen(arrived[2])]
    later, one = lax.optimization_barrier((later, one))
    two = narrow(expert_call(quarter, later, [factors[3], factors[2]], *weights))
    low, high = slice(0, slot_count), slice(slot_count, 2 * slot_count)
    back = [None] * depth
    back[1] = shift(add(one[0, high], over(one[1, high])), -1)
    back[0] = add(one[0, low], over(one[1, low]))
    back[2] = shift(add(two[0, high], over(two[1, high])), -2)
    back[3] = shift(add(two[0, low], over(two[1, low])), -3)
    return lax.dot_general(
        placing,
        jnp.concatenate(back, axis=0),
        (((1,), (0,)), ((), ())),
        preferred_element_type=jnp.float32,
    )


def gathered_experts(gained, inverse, expert_ids, expert_slots, slot_count, gate_w, up_w, down_w):
    expert_in = (gained * inverse).astype(jnp.bfloat16)
    experts = gate_w.shape[0] * lax.axis_size("ba")
    combined = expert_ids * slot_count + expert_slots
    placing = (
        combined[:, None] == lax.broadcasted_iota(jnp.int32, (1, experts * slot_count), 1)
    ) & (expert_slots[:, None] >= 0)
    placing = placing.astype(jnp.bfloat16)
    packed = lax.dot_general(
        placing, expert_in, (((0,), (0,)), ((), ())), preferred_element_type=jnp.float32
    ).astype(jnp.bfloat16)
    arrived = lax.all_to_all(packed, "ba", split_axis=0, concat_axis=0, tiled=True)
    piece = lax.all_gather(arrived, "aa", axis=1, tiled=True)
    gate_part = jnp.dot(piece, gate_w[0], preferred_element_type=jnp.float32)
    up_part = jnp.dot(piece, up_w[0], preferred_element_type=jnp.float32)
    act = (jax.nn.silu(gate_part) * up_part).astype(jnp.bfloat16)
    expert_out = lax.psum_scatter(
        lax.dot_general(
            down_w[0], act, (((0,), (1,)), ((), ())), preferred_element_type=jnp.float32
        ).astype(jnp.bfloat16),
        "aa",
        scatter_dimension=0,
        tiled=True,
    )
    returned = lax.all_to_all(expert_out, "ba", split_axis=1, concat_axis=1, tiled=True)
    return lax.dot_general(
        placing, returned, (((1,), (1,)), ((), ())), preferred_element_type=jnp.float32
    )


def on_device(
    query,
    keys,
    values,
    cache_lengths,
    residual,
    out_weight,
    norm_gain,
    router_weight,
    expert_ids,
    expert_slots,
    expert_gate,
    expert_up,
    expert_down,
):
    square = lax.axis_size("aa") == 4 and lax.axis_size("ba") == 4
    split = (
        square
        and keys.shape[1] == 2 * HD
        and keys.shape[0] % KEY_BLOCK == 0
        and query.shape[0] == residual.shape[0]
    )
    project = split_projection if split else plain_projection
    hidden = residual.astype(jnp.float32) + project(
        query, keys, values, cache_lengths, out_weight
    )
    width = hidden.shape[1] * lax.axis_size("aa")
    experts = router_weight.shape[1]
    gained = hidden * norm_gain
    squares = jnp.sum(hidden * hidden, axis=1, keepdims=True)
    raw = jnp.dot(gained, router_weight, precision=lax.Precision.HIGHEST)
    sums = lax.psum(jnp.concatenate([squares, raw], axis=1), "aa")
    inverse = 1.0 / jnp.sqrt(sums[:, :1] / width + EPSILON)
    logits = sums[:, 1:] * inverse
    chosen = expert_ids[:, None] == lax.broadcasted_iota(jnp.int32, (1, experts), 1)
    gate = jnp.sum(jnp.where(chosen, jax.nn.sigmoid(logits), 0.0), axis=1)
    slot_count = 2 * query.shape[0] * lax.axis_size("aa") // (lax.axis_size("ba") * experts)
    run = routed_experts if square and expert_gate.shape[0] == 1 else gathered_experts
    from_experts = run(
        gained, inverse, expert_ids, expert_slots, slot_count, expert_gate, expert_up, expert_down
    )
    return (hidden + gate[:, None] * from_experts).astype(jnp.bfloat16)


def solution(mesh):
    return jax.shard_map(
        on_device,
        mesh=mesh,
        in_specs=(
            P(("ga", "aa"), "ba"),
            P(("ga", "aa"), "ba"),
            P(("ga", "aa"), "ba"),
            P(("ga", "aa")),
            P(("ga", "ba"), "aa"),
            P("ba", "aa"),
            P("aa"),
            P("aa", None),
            P(("ga", "ba")),
            P(("ga", "ba")),
            P("ba", None, "aa"),
            P("ba", None, "aa"),
            P("ba", "aa", None),
        ),
        out_specs=P(("ga", "ba"), "aa"),
        check_vma=False,
    )
```

```python
import functools
import math

import jax
import jax.numpy as jnp
from jax import lax
from jax.experimental import pallas as pl
from jax.experimental.pallas import tpu as pltpu
from jax.sharding import PartitionSpec as P

HD = 128
KEY_BLOCK = 1024
STEP = 256
MARKS = 32
SMALL_VMEM = 16 * 1024 * 1024
EXPERT_VMEM = 52 * 1024 * 1024
TOKEN = jax.ShapeDtypeStruct((8, HD), jnp.float32)
LIGHT = pl.CostEstimate(flops=1000, bytes_accessed=1000, transcendentals=0)
NEGATIVE = -1e30
EPSILON = 1e-05
SCALE = HD ** (-0.5)
SCALE_LOG2 = SCALE * math.log2(math.e)


def head_partials(rows, key_block, value_block, length):
    heads = rows.shape[1] // HD
    kv_heads = key_block.shape[1] // HD
    group = heads // kv_heads
    valid = lax.broadcasted_iota(jnp.int32, (1, key_block.shape[0]), 1) < length
    maxima = []
    totals = []
    outputs = []
    for head in range(heads):
        source = head // group
        q_head = rows[:, head * HD : (head + 1) * HD]
        k_head = key_block[:, source * HD : (source + 1) * HD]
        v_head = value_block[:, source * HD : (source + 1) * HD]
        scores = lax.dot_general(
            q_head, k_head, (((1,), (1,)), ((), ())), preferred_element_type=jnp.float32
        ) * SCALE
        scores = jnp.where(valid, scores, NEGATIVE)
        peak = jnp.max(scores, axis=1)
        probs = jnp.exp(scores - peak[:, None])
        maxima.append(peak)
        totals.append(jnp.sum(probs, axis=1))
        outputs.append(
            jnp.dot(probs.astype(jnp.bfloat16), v_head, preferred_element_type=jnp.float32)
        )
    return (jnp.stack(maxima, axis=1), jnp.stack(totals, axis=1), jnp.concatenate(outputs, axis=1))


def combine_partials(first, second):
    peak_one, total_one, out_one = first
    peak_two, total_two, out_two = second
    peak = jnp.maximum(peak_one, peak_two)
    scale_one = jnp.exp(peak_one - peak)
    scale_two = jnp.exp(peak_two - peak)
    outputs = out_one * jnp.repeat(scale_one, HD, axis=1) + out_two * jnp.repeat(
        scale_two, HD, axis=1
    )
    return (peak, total_one * scale_one + total_two * scale_two, outputs)


def plain_projection(query, keys, values, cache_lengths, out_weight):
    heads = query.shape[1] // HD
    own_rows = query.shape[0]
    context = keys.shape[0]
    start_state = (
        jnp.full((own_rows, heads), NEGATIVE, jnp.float32),
        jnp.zeros((own_rows, heads), jnp.float32),
        jnp.zeros((own_rows, heads * HD), jnp.float32),
    )
    key_piece = lax.all_gather(keys, "aa", axis=0, tiled=True)
    value_piece = lax.all_gather(values, "aa", axis=0, tiled=True)
    length_piece = lax.all_gather(cache_lengths, "aa", axis=0, tiled=True)

    def one_shard(index, carry):
        key_block = lax.dynamic_slice_in_dim(key_piece, index * context, context, 0)
        value_block = lax.dynamic_slice_in_dim(value_piece, index * context, context, 0)
        return combine_partials(
            carry, head_partials(query, key_block, value_block, length_piece[index])
        )

    peak, total, weighted = lax.fori_loop(0, length_piece.shape[0], one_shard, start_state)
    own = (weighted / jnp.repeat(total, HD, axis=1)).astype(jnp.bfloat16)
    attended = lax.all_gather(own, "aa", axis=0, tiled=True)
    return lax.psum_scatter(
        jnp.dot(attended, out_weight, preferred_element_type=jnp.float32).astype(jnp.bfloat16),
        "ba",
        scatter_dimension=0,
        tiled=True,
    ).astype(jnp.float32)


def prepare_body(scalars, q_ref, k_ref, v_ref, own_query, far_query, own_cache, far_cache, marks, sems):
    side, length = scalars[0], scalars[1]
    context = k_ref.shape[0]
    half = own_query.shape[1]
    rows = MARKS // 2
    marks[:rows] = jnp.full((rows, 2 * HD), length // 256, jnp.int32).astype(jnp.float32).astype(jnp.bfloat16)
    marks[rows:] = jnp.full((rows, 2 * HD), lax.rem(length, 256), jnp.int32).astype(jnp.float32).astype(jnp.bfloat16)
    copies = []
    for query_out, cache_out, which in (
        (far_query, far_cache, 1 - side),
        (own_query, own_cache, side),
    ):
        column = pl.ds(pl.multiple_of(which * HD, HD), HD)
        for source, target in (
            (q_ref.at[:, pl.ds(pl.multiple_of(which * half, HD), half)], query_out),
            (k_ref.at[:, column], cache_out.at[pl.ds(0, context), pl.ds(0, HD)]),
            (v_ref.at[:, column], cache_out.at[pl.ds(0, context), pl.ds(HD, HD)]),
            (marks, cache_out.at[pl.ds(context, MARKS), :]),
        ):
            copy = pltpu.make_async_copy(source, target, sems.at[len(copies)])
            copy.start()
            copies.append(copy)
    for copy in copies:
        copy.wait()


def prepare(side, cache_lengths, query, keys, values):
    scalars = jnp.concatenate([side[None].astype(jnp.int32), cache_lengths])
    hbm = pl.BlockSpec(memory_space=pltpu.HBM)
    half = jax.ShapeDtypeStruct((query.shape[0], query.shape[1] // 2), jnp.bfloat16)
    cache = jax.ShapeDtypeStruct((keys.shape[0] + MARKS, 2 * HD), jnp.bfloat16)
    return pl.pallas_call(
        prepare_body,
        out_shape=(half, half, cache, cache),
        in_specs=[pl.BlockSpec(memory_space=pltpu.SMEM), hbm, hbm, hbm],
        out_specs=(hbm, hbm, hbm, hbm),
        scratch_shapes=[
            pltpu.VMEM((MARKS, 2 * HD), jnp.bfloat16),
            pltpu.SemaphoreType.DMA((8,)),
        ],
        compiler_params=pltpu.CompilerParams(vmem_limit_bytes=SMALL_VMEM),
    )(scalars, query, keys, values)


def after_body(*refs):
    pass


def after(value, *others):
    anywhere = pl.BlockSpec(memory_space=pl.ANY)
    return pl.pallas_call(
        after_body,
        out_shape=jax.ShapeDtypeStruct(value.shape, value.dtype),
        in_specs=[anywhere] * (1 + len(others)),
        out_specs=anywhere,
        input_output_aliases={0: 0},
        compiler_params=pltpu.CompilerParams(vmem_limit_bytes=SMALL_VMEM),
        cost_estimate=LIGHT,
    )(value, *others)


def attend_body(*refs, shards, units, resume, finish, ordered, block):
    q_ref = refs[0]
    kv_refs = refs[1 : 1 + shards]
    at = 1 + shards
    if resume:
        peak_in, sums_in = refs[at : at + 2]
        at += 2
    at += ordered
    if finish:
        out_ref, token, peak, sums, held, sems = refs[at : at + 6]
    else:
        peak, sums, token, held, sems = refs[at : at + 5]
    copies = [
        pltpu.make_async_copy(kv_refs[shard], held.at[shard], sems.at[shard])
        for shard in range(shards)
    ]
    for copy in copies:
        copy.start()
    token[...] = jnp.zeros(token.shape, jnp.float32)
    if resume:
        peak[...] = peak_in[...]
        sums[...] = sums_in[...]
    else:
        peak[...] = jnp.full(peak.shape, NEGATIVE, jnp.float32)
        sums[...] = jnp.zeros(sums.shape, jnp.float32)

    def one_block(shard, base, length, high, tail):
        key = held[shard, pl.ds(base, high), :HD]
        value = held[shard, pl.ds(base, high), HD:]
        ones = jnp.ones((high, HD), jnp.bfloat16)
        if tail:
            valid = base + lax.broadcasted_iota(jnp.int32, (high, HD), 0) < length
            first = held[shard, 0:16, :HD].astype(jnp.float32)[0:1]
            key = jnp.where(valid, key.astype(jnp.float32), first).astype(jnp.bfloat16)
            value = jnp.where(valid, value.astype(jnp.float32), 0.0).astype(jnp.bfloat16)
            ones = jnp.where(valid, 1.0, 0.0).astype(jnp.bfloat16)
        value = jnp.concatenate([value, ones], axis=1)

        def score(unit):
            return lax.dot_general(
                q_ref[:, unit * HD : (unit + 1) * HD],
                key,
                (((1,), (1,)), ((), ())),
                preferred_element_type=jnp.float32,
            )

        following = score(0)
        for unit in range(units):
            scores = following
            if unit + 1 < units:
                following = score(unit + 1)
            before = peak[unit]
            top = jnp.maximum(before, jnp.max(scores, axis=1, keepdims=True))
            peak[unit] = top
            probs = jnp.exp2(
                (scores - jnp.concatenate([top] * (high // HD), axis=1)) * SCALE_LOG2
            ).astype(jnp.bfloat16)
            fade = jnp.exp2((before - top) * SCALE_LOG2)
            sums[unit] = sums[unit] * jnp.concatenate([fade, fade], axis=1) + jnp.dot(
                probs, value, preferred_element_type=jnp.float32
            )

    context = held.shape[1] - MARKS

    @pl.loop(0, shards)
    def _(shard):
        for at, copy in enumerate(copies):

            @pl.when(shard == at)
            def _(copy=copy):
                copy.wait()

        marks = jnp.max(
            held[shard, context : context + MARKS, :HD]
            .astype(jnp.float32)
            .reshape(2, MARKS // 2, HD),
            axis=1,
        ).astype(jnp.int32)
        length = jnp.max(marks[0:1]) * 256 + jnp.max(marks[1:2])
        whole = length // block
        left = length - whole * block

        @pl.loop(0, whole)
        def _(step):
            one_block(shard, pl.multiple_of(step * block, block), length, block, False)

        for high in range(STEP, block + 1, STEP):

            @pl.when(jnp.logical_and(left > high - STEP, left <= high))
            def _(high=high):
                one_block(shard, pl.multiple_of(whole * block, block), length, high, True)

    if finish:
        for unit in range(units):
            total = sums[unit]
            out_ref[:, unit * HD : (unit + 1) * HD] = (total[:, :HD] / total[:, HD:]).astype(
                jnp.bfloat16
            )


def attend(query, caches, state=None, finish=False, behind=None):
    rows, width = query.shape
    units = width // HD
    shards = len(caches)
    peak = jax.ShapeDtypeStruct((units, rows, HD), jnp.float32)
    sums = jax.ShapeDtypeStruct((units, rows, 2 * HD), jnp.float32)
    vmem = pl.BlockSpec(memory_space=pltpu.VMEM)
    operands = [query, *caches]
    if state is not None:
        operands += list(state)
    if finish:
        out_shape = (jax.ShapeDtypeStruct(query.shape, jnp.bfloat16), TOKEN)
        scratch = [pltpu.VMEM(peak.shape, peak.dtype), pltpu.VMEM(sums.shape, sums.dtype)]
    else:
        out_shape = (peak, sums, TOKEN)
        scratch = []
    in_specs = [vmem] * len(operands)
    in_specs[1 : 1 + shards] = [pl.BlockSpec(memory_space=pltpu.HBM)] * shards
    scratch += [
        pltpu.VMEM((shards, *caches[0].shape), jnp.bfloat16),
        pltpu.SemaphoreType.DMA((shards,)),
    ]
    if behind is not None:
        operands.append(behind)
        in_specs.append(pl.BlockSpec(memory_space=pl.ANY))
    return pl.pallas_call(
        functools.partial(
            attend_body,
            shards=shards,
            units=units,
            resume=state is not None,
            finish=finish,
            ordered=behind is not None,
            block=KEY_BLOCK,
        ),
        out_shape=out_shape,
        in_specs=in_specs,
        out_specs=(vmem,) * len(out_shape),
        scratch_shapes=scratch,
        compiler_params=pltpu.CompilerParams(vmem_limit_bytes=SMALL_VMEM),
        cost_estimate=LIGHT,
    )(*operands)


def swap_pairs(size, mask):
    return [(index, index ^ mask) for index in range(size)]


def add(one, two):
    return (one.astype(jnp.float32) + two.astype(jnp.float32)).astype(jnp.bfloat16)


def split_projection(query, keys, values, cache_lengths, out_weight):
    size = lax.axis_size("aa")
    index = lax.axis_index("aa")
    side = index // 2
    over = functools.partial(lax.ppermute, axis_name="aa", perm=swap_pairs(size, 2))
    core = functools.partial(lax.ppermute, axis_name="aa", perm=swap_pairs(size, 1))
    half = query.shape[1] // 2

    own_query, away_query, own_cache, away_cache = prepare(
        side, cache_lengths, query, keys, values
    )
    far_query = over(away_query)
    far_cache = over(away_cache)
    near_cache = core(own_cache)
    *own_state, token = attend(own_query, [own_cache, near_cache])
    far_cache = after(far_cache, token)
    corner_cache = core(far_cache)
    own_rows, token = attend(own_query, [far_cache, corner_cache], own_state, True)
    far_other = over(own_rows)
    *far_state, token = attend(far_query, [own_cache, near_cache], behind=token)
    far_rows, token = attend(
        far_query, [far_cache, corner_cache], far_state, True, behind=far_other
    )
    own_other = over(far_rows)
    first = jnp.stack([own_rows, far_rows, core(own_rows), core(far_rows)])
    second = jnp.stack([own_other, far_other, core(own_other), core(far_other)])
    first_weight = lax.dynamic_slice_in_dim(out_weight, side * half, half, 0)
    second_weight = lax.dynamic_slice_in_dim(out_weight, (1 - side) * half, half, 0)

    place = lax.axis_index("ba")
    low = place < 2
    order = (jnp.where(low, 3, 0), jnp.where(low, 2, 1), place ^ 1, place)
    columns = out_weight.shape[1]
    cut = columns // 2 if columns % (2 * HD) == 0 else columns

    def product(step, begin):
        mask = index ^ order[step]
        slot = mask // 2 + 2 * (mask % 2)
        left = lax.dynamic_index_in_dim(first, slot, 0, False)
        right = lax.dynamic_index_in_dim(second, slot, 0, False)
        return jnp.dot(
            left, first_weight[:, begin : begin + cut], preferred_element_type=jnp.float32
        ) + jnp.dot(
            right, second_weight[:, begin : begin + cut], preferred_element_type=jnp.float32
        )

    send = functools.partial(lax.ppermute, axis_name="ba")
    starts = range(0, columns, cut)
    one = [product(0, begin).astype(jnp.bfloat16) for begin in starts]
    up = [send(part, perm=[(0, 1), (3, 2)]) for part in one]
    down = list(up)
    two = [product(1, begin).astype(jnp.bfloat16) for begin in starts]
    for at in range(len(one)):
        up[at] = send(
            add(jnp.where(place == 0, two[at], one[at]), up[at]), perm=[(0, 1), (1, 2)]
        )
        down[at] = send(
            add(jnp.where(place == 3, two[at], one[at]), down[at]), perm=[(3, 2), (2, 1)]
        )
    three = [product(2, begin).astype(jnp.bfloat16) for begin in starts]
    for at in range(len(one)):
        up[at] = send(
            add(jnp.where(place == 1, two[at], three[at]), up[at]),
            perm=[(0, 1), (1, 2), (2, 3)],
        )
        down[at] = send(
            add(jnp.where(place == 2, two[at], three[at]), down[at]),
            perm=[(3, 2), (2, 1), (1, 0)],
        )
    return jnp.concatenate(
        [
            product(3, begin) + up[at].astype(jnp.float32) + down[at].astype(jnp.float32)
            for at, begin in enumerate(starts)
        ],
        axis=1,
    )


def expert_body(quarter, *refs, blocks, ordered, tile):
    piece_refs = refs[: 4 * blocks]
    gate_hbm, up_hbm, down_hbm = refs[4 * blocks : 4 * blocks + 3]
    out_ref, token, gate_w, up_w, down_w, gate_sum, up_sum, act, sems = refs[
        4 * blocks + 3 + ordered :
    ]
    _, width, hidden_units = gate_w.shape
    inward, outward = [], []
    for piece in range(4):
        at = pl.ds(pl.multiple_of(quarter[piece] * width, HD), width)
        inward.append(
            [
                pltpu.make_async_copy(gate_hbm.at[0, at, :], gate_w.at[piece], sems.at[0, piece]),
                pltpu.make_async_copy(up_hbm.at[0, at, :], up_w.at[piece], sems.at[1, piece]),
            ]
        )
        outward.append(
            pltpu.make_async_copy(down_hbm.at[0, :, at], down_w.at[piece], sems.at[2, piece])
        )
    for pair in inward:
        for copy in pair:
            copy.start()
    for copy in outward:
        copy.start()
    token[...] = jnp.zeros(token.shape, jnp.float32)
    factors = []
    for block in range(blocks):
        total = 0.0
        for piece in range(4):
            total += jnp.sum(
                piece_refs[4 * block + piece][:, width:].astype(jnp.float32), axis=1, keepdims=True
            )
        factors.append(1.0 / jnp.sqrt(total / (4 * width) + EPSILON))
    scale = jnp.concatenate(factors, axis=0)
    for piece in range(4):
        operand = jnp.concatenate(
            [piece_refs[4 * block + piece][:, :width] for block in range(blocks)], axis=0
        )
        for copy, weight, total in zip(inward[piece], (gate_w, up_w), (gate_sum, up_sum)):
            copy.wait()
            for begin in range(0, hidden_units, tile):
                columns = slice(begin, begin + tile)
                part = jnp.dot(
                    operand, weight[piece, :, columns], preferred_element_type=jnp.float32
                )
                if piece > 0:
                    part += total[:, columns]
                total[:, columns] = part
    for begin in range(0, hidden_units, tile):
        columns = slice(begin, begin + tile)
        gate_part = gate_sum[:, columns] * scale
        act[:, columns] = (
            gate_part / (1.0 + jnp.exp(-gate_part)) * (up_sum[:, columns] * scale)
        ).astype(jnp.bfloat16)
    for piece in range(4):
        outward[piece].wait()
        for begin in range(0, width, tile):
            columns = slice(begin, begin + tile)
            out_ref[piece, :, columns] = jnp.dot(
                act[...], down_w[piece, :, columns], preferred_element_type=jnp.float32
            ).astype(jnp.bfloat16)


def expert_call(quarter, pieces, gate_w, up_w, down_w, behind=None):
    blocks = len(pieces)
    rows = pieces[0][0].shape[0]
    width = gate_w.shape[1] // 4
    hidden_units = gate_w.shape[2]
    high = blocks * rows
    vmem = pl.BlockSpec(memory_space=pltpu.VMEM)
    flat = [piece for block in pieces for piece in block]
    operands = [quarter, *flat, gate_w, up_w, down_w]
    in_specs = [pl.BlockSpec(memory_space=pltpu.SMEM)] + [vmem] * len(flat)
    in_specs += [pl.BlockSpec(memory_space=pltpu.HBM)] * 3
    if behind is not None:
        operands.append(behind)
        in_specs.append(pl.BlockSpec(memory_space=pl.ANY))
    return pl.pallas_call(
        functools.partial(expert_body, blocks=blocks, ordered=behind is not None, tile=2 * HD),
        in_specs=in_specs,
        out_specs=(vmem, vmem),
        out_shape=(jax.ShapeDtypeStruct((4, high, width), jnp.bfloat16), TOKEN),
        scratch_shapes=[
            pltpu.VMEM((4, width, hidden_units), jnp.bfloat16),
            pltpu.VMEM((4, width, hidden_units), jnp.bfloat16),
            pltpu.VMEM((4, hidden_units, width), jnp.bfloat16),
            pltpu.VMEM((high, hidden_units), jnp.float32),
            pltpu.VMEM((high, hidden_units), jnp.float32),
            pltpu.VMEM((high, hidden_units), jnp.bfloat16),
            pltpu.SemaphoreType.DMA((3, 4)),
        ],
        compiler_params=pltpu.CompilerParams(vmem_limit_bytes=EXPERT_VMEM),
        cost_estimate=LIGHT,
    )(*operands)


def routed_experts(
    gained, squares, stats, expert_ids, expert_slots, slot_count, gate_w, up_w, down_w
):
    size = lax.axis_size("aa")
    index = lax.axis_index("aa")
    depth = lax.axis_size("ba")
    place = lax.axis_index("ba")
    over = functools.partial(lax.ppermute, axis_name="aa", perm=swap_pairs(size, 2))
    core = functools.partial(lax.ppermute, axis_name="aa", perm=swap_pairs(size, 1))

    def shift(array, by):
        return lax.ppermute(
            array, "ba", perm=[(at, (at + by) % depth) for at in range(depth)]
        )

    ahead = lax.rem(expert_ids - place + depth, depth)
    combined = ahead * slot_count + expert_slots
    chosen = (
        combined[:, None] == lax.broadcasted_iota(jnp.int32, (1, depth * slot_count), 1)
    ) & (expert_slots[:, None] >= 0)
    placing = chosen.astype(jnp.bfloat16)
    coarse = squares.astype(jnp.bfloat16)
    fine = (squares - coarse.astype(jnp.float32)).astype(jnp.bfloat16)
    rows = jnp.concatenate(
        [
            gained.astype(jnp.bfloat16),
            coarse,
            fine,
            jnp.zeros((gained.shape[0], HD - 2), jnp.bfloat16),
        ],
        axis=1,
    )
    slots = [slice(at * slot_count, (at + 1) * slot_count) for at in range(depth)]
    parts = [
        lax.dot_general(
            placing[:, slots[at]], rows, (((0,), (0,)), ((), ())), preferred_element_type=jnp.float32
        ).astype(jnp.bfloat16)
        for at in range(depth)
    ]

    def widen(block, far=None):
        far = over(block) if far is None else far
        both = core(jnp.stack([block, far]))
        return [block, far, both[0], both[1]]

    arrived = [parts[0], shift(parts[1], 1), None, shift(parts[3], 3)]
    arrived[2] = shift(parts[2], 2)
    quarter = jnp.stack([index, index ^ 2, index ^ 1, index ^ 3]).astype(jnp.int32)

    def narrow(share):
        return add(share[:2], core(share[2:]))

    weights = (gate_w, up_w, down_w)
    one, token = expert_call(quarter, [widen(arrived[0]), widen(arrived[1])], *weights)
    stats = after(stats.T, token)
    stats = stats + core(stats)
    stats = (stats + over(stats)).T
    one = narrow(one)
    low, high = slice(0, slot_count), slice(slot_count, 2 * slot_count)
    third = widen(arrived[3], after(over(arrived[3]), token))
    second = widen(after(arrived[2], token))
    two, token = expert_call(quarter, [third, second], *weights)
    two = narrow(two)
    back = [None] * depth
    crossed = over(two[1, high])
    back[2] = shift(add(two[0, high], crossed), -2)
    back[3] = shift(add(two[0, low], over(two[1, low])), -3)
    near = over(after(one, crossed)[1, high])
    back[1] = shift(add(one[0, high], near), -1)
    back[0] = add(one[0, low], over(after(one, near)[1, low]))
    return lax.dot_general(
        placing,
        jnp.concatenate(back, axis=0),
        (((1,), (0,)), ((), ())),
        preferred_element_type=jnp.float32,
    ), stats


def gathered_experts(
    gained, squares, stats, expert_ids, expert_slots, slot_count, gate_w, up_w, down_w
):
    stats = lax.psum(stats, "aa")
    width = gained.shape[1] * lax.axis_size("aa")
    inverse = 1.0 / jnp.sqrt(stats[:, :1] / width + EPSILON)
    expert_in = (gained * inverse).astype(jnp.bfloat16)
    experts = gate_w.shape[0] * lax.axis_size("ba")
    combined = expert_ids * slot_count + expert_slots
    placing = (
        combined[:, None] == lax.broadcasted_iota(jnp.int32, (1, experts * slot_count), 1)
    ) & (expert_slots[:, None] >= 0)
    placing = placing.astype(jnp.bfloat16)
    packed = lax.dot_general(
        placing, expert_in, (((0,), (0,)), ((), ())), preferred_element_type=jnp.float32
    ).astype(jnp.bfloat16)
    arrived = lax.all_to_all(packed, "ba", split_axis=0, concat_axis=0, tiled=True)
    piece = lax.all_gather(arrived, "aa", axis=1, tiled=True)
    gate_part = jnp.dot(piece, gate_w[0], preferred_element_type=jnp.float32)
    up_part = jnp.dot(piece, up_w[0], preferred_element_type=jnp.float32)
    act = (jax.nn.silu(gate_part) * up_part).astype(jnp.bfloat16)
    expert_out = lax.psum_scatter(
        lax.dot_general(
            down_w[0], act, (((0,), (1,)), ((), ())), preferred_element_type=jnp.float32
        ).astype(jnp.bfloat16),
        "aa",
        scatter_dimension=0,
        tiled=True,
    )
    returned = lax.all_to_all(expert_out, "ba", split_axis=1, concat_axis=1, tiled=True)
    return lax.dot_general(
        placing, returned, (((1,), (1,)), ((), ())), preferred_element_type=jnp.float32
    ), stats


def on_device(
    query,
    keys,
    values,
    cache_lengths,
    residual,
    out_weight,
    norm_gain,
    router_weight,
    expert_ids,
    expert_slots,
    expert_gate,
    expert_up,
    expert_down,
):
    square = lax.axis_size("aa") == 4 and lax.axis_size("ba") == 4
    split = (
        square
        and keys.shape[1] == 2 * HD
        and keys.shape[0] % KEY_BLOCK == 0
        and query.shape[0] == residual.shape[0]
    )
    project = split_projection if split else plain_projection
    hidden = residual.astype(jnp.float32) + project(
        query, keys, values, cache_lengths, out_weight
    )
    width = hidden.shape[1] * lax.axis_size("aa")
    experts = router_weight.shape[1]
    gained = hidden * norm_gain
    squares = jnp.sum(hidden * hidden, axis=1, keepdims=True)
    raw = jnp.dot(gained, router_weight, precision=lax.Precision.HIGHEST)
    stats = jnp.concatenate([squares, raw], axis=1)

    slot_count = 2 * query.shape[0] * lax.axis_size("aa") // (lax.axis_size("ba") * experts)
    run = routed_experts if square and expert_gate.shape[0] == 1 else gathered_experts
    from_experts, sums = run(
        gained,
        squares,
        stats,
        expert_ids,
        expert_slots,
        slot_count,
        expert_gate,
        expert_up,
        expert_down,
    )
    logits = sums[:, 1:] / jnp.sqrt(sums[:, :1] / width + EPSILON)
    chosen = expert_ids[:, None] == lax.broadcasted_iota(jnp.int32, (1, experts), 1)
    gate = jnp.sum(jnp.where(chosen, jax.nn.sigmoid(logits), 0.0), axis=1)
    return (hidden + gate[:, None] * from_experts).astype(jnp.bfloat16)


def solution(mesh):
    return jax.shard_map(
        on_device,
        mesh=mesh,
        in_specs=(
            P(("ga", "aa"), "ba"),
            P(("ga", "aa"), "ba"),
            P(("ga", "aa"), "ba"),
            P(("ga", "aa")),
            P(("ga", "ba"), "aa"),
            P("ba", "aa"),
            P("aa"),
            P("aa", None),
            P(("ga", "ba")),
            P(("ga", "ba")),
            P("ba", None, "aa"),
            P("ba", None, "aa"),
            P("ba", "aa", None),
        ),
        out_specs=P(("ga", "ba"), "aa"),
        check_vma=False,
    )
```

```python
import functools
import math

import jax
import jax.numpy as jnp
from jax import lax
from jax.experimental import pallas as pl
from jax.experimental.pallas import tpu as pltpu
from jax.sharding import PartitionSpec as P

HD = 128
KEY_BLOCK = 1024
MARKS = 32
SMALL_VMEM = 16 * 1024 * 1024
EXPERT_VMEM = 52 * 1024 * 1024
TOKEN = jax.ShapeDtypeStruct((8, HD), jnp.float32)
LIGHT = pl.CostEstimate(flops=1000, bytes_accessed=1000, transcendentals=0)
NEGATIVE = -1e30
EPSILON = 1e-05
SCALE = HD ** (-0.5)
SCALE_LOG2 = SCALE * math.log2(math.e)


def head_partials(rows, key_block, value_block, length):
    heads = rows.shape[1] // HD
    kv_heads = key_block.shape[1] // HD
    group = heads // kv_heads
    valid = lax.broadcasted_iota(jnp.int32, (1, key_block.shape[0]), 1) < length
    maxima = []
    totals = []
    outputs = []
    for head in range(heads):
        source = head // group
        q_head = rows[:, head * HD : (head + 1) * HD]
        k_head = key_block[:, source * HD : (source + 1) * HD]
        v_head = value_block[:, source * HD : (source + 1) * HD]
        scores = lax.dot_general(
            q_head, k_head, (((1,), (1,)), ((), ())), preferred_element_type=jnp.float32
        ) * SCALE
        scores = jnp.where(valid, scores, NEGATIVE)
        peak = jnp.max(scores, axis=1)
        probs = jnp.exp(scores - peak[:, None])
        maxima.append(peak)
        totals.append(jnp.sum(probs, axis=1))
        outputs.append(
            jnp.dot(probs.astype(jnp.bfloat16), v_head, preferred_element_type=jnp.float32)
        )
    return (jnp.stack(maxima, axis=1), jnp.stack(totals, axis=1), jnp.concatenate(outputs, axis=1))


def combine_partials(first, second):
    peak_one, total_one, out_one = first
    peak_two, total_two, out_two = second
    peak = jnp.maximum(peak_one, peak_two)
    scale_one = jnp.exp(peak_one - peak)
    scale_two = jnp.exp(peak_two - peak)
    outputs = out_one * jnp.repeat(scale_one, HD, axis=1) + out_two * jnp.repeat(
        scale_two, HD, axis=1
    )
    return (peak, total_one * scale_one + total_two * scale_two, outputs)


def plain_projection(query, keys, values, cache_lengths, out_weight):
    heads = query.shape[1] // HD
    own_rows = query.shape[0]
    context = keys.shape[0]
    start_state = (
        jnp.full((own_rows, heads), NEGATIVE, jnp.float32),
        jnp.zeros((own_rows, heads), jnp.float32),
        jnp.zeros((own_rows, heads * HD), jnp.float32),
    )
    key_piece = lax.all_gather(keys, "aa", axis=0, tiled=True)
    value_piece = lax.all_gather(values, "aa", axis=0, tiled=True)
    length_piece = lax.all_gather(cache_lengths, "aa", axis=0, tiled=True)

    def one_shard(index, carry):
        key_block = lax.dynamic_slice_in_dim(key_piece, index * context, context, 0)
        value_block = lax.dynamic_slice_in_dim(value_piece, index * context, context, 0)
        return combine_partials(
            carry, head_partials(query, key_block, value_block, length_piece[index])
        )

    peak, total, weighted = lax.fori_loop(0, length_piece.shape[0], one_shard, start_state)
    own = (weighted / jnp.repeat(total, HD, axis=1)).astype(jnp.bfloat16)
    attended = lax.all_gather(own, "aa", axis=0, tiled=True)
    return lax.psum_scatter(
        jnp.dot(attended, out_weight, preferred_element_type=jnp.float32).astype(jnp.bfloat16),
        "ba",
        scatter_dimension=0,
        tiled=True,
    ).astype(jnp.float32)


def prepare_body(scalars, q_ref, k_ref, v_ref, own_query, far_query, own_cache, far_cache, marks, sems):
    side, length = scalars[0], scalars[1]
    context = k_ref.shape[0]
    half = own_query.shape[1]
    rows = MARKS // 2
    marks[:rows] = jnp.full((rows, 2 * HD), length // 256, jnp.int32).astype(jnp.float32).astype(jnp.bfloat16)
    marks[rows:] = jnp.full((rows, 2 * HD), lax.rem(length, 256), jnp.int32).astype(jnp.float32).astype(jnp.bfloat16)
    copies = []
    for query_out, cache_out, which in (
        (far_query, far_cache, 1 - side),
        (own_query, own_cache, side),
    ):
        column = pl.ds(pl.multiple_of(which * HD, HD), HD)
        for source, target in (
            (q_ref.at[:, pl.ds(pl.multiple_of(which * half, HD), half)], query_out),
            (k_ref.at[:, column], cache_out.at[pl.ds(0, context), pl.ds(0, HD)]),
            (v_ref.at[:, column], cache_out.at[pl.ds(0, context), pl.ds(HD, HD)]),
            (marks, cache_out.at[pl.ds(context, MARKS), :]),
        ):
            copy = pltpu.make_async_copy(source, target, sems.at[len(copies)])
            copy.start()
            copies.append(copy)
    for copy in copies:
        copy.wait()


def prepare(side, cache_lengths, query, keys, values):
    scalars = jnp.concatenate([side[None].astype(jnp.int32), cache_lengths])
    hbm = pl.BlockSpec(memory_space=pltpu.HBM)
    half = jax.ShapeDtypeStruct((query.shape[0], query.shape[1] // 2), jnp.bfloat16)
    cache = jax.ShapeDtypeStruct((keys.shape[0] + MARKS, 2 * HD), jnp.bfloat16)
    return pl.pallas_call(
        prepare_body,
        out_shape=(half, half, cache, cache),
        in_specs=[pl.BlockSpec(memory_space=pltpu.SMEM), hbm, hbm, hbm],
        out_specs=(hbm, hbm, hbm, hbm),
        scratch_shapes=[
            pltpu.VMEM((MARKS, 2 * HD), jnp.bfloat16),
            pltpu.SemaphoreType.DMA((8,)),
        ],
        compiler_params=pltpu.CompilerParams(vmem_limit_bytes=SMALL_VMEM),
    )(scalars, query, keys, values)


def after_body(*refs):
    pass


def after(value, *others):
    anywhere = pl.BlockSpec(memory_space=pl.ANY)
    return pl.pallas_call(
        after_body,
        out_shape=jax.ShapeDtypeStruct(value.shape, value.dtype),
        in_specs=[anywhere] * (1 + len(others)),
        out_specs=anywhere,
        input_output_aliases={0: 0},
        compiler_params=pltpu.CompilerParams(vmem_limit_bytes=SMALL_VMEM),
        cost_estimate=LIGHT,
    )(value, *others)


def attend_body(*refs, shards, units, resume, finish, ordered, block):
    q_ref = refs[0]
    kv_refs = refs[1 : 1 + shards]
    at = 1 + shards
    if resume:
        peak_in, sums_in = refs[at : at + 2]
        at += 2
    at += ordered
    if finish:
        out_ref, token, peak, sums, held, sems = refs[at : at + 6]
    else:
        peak, sums, token, held, sems = refs[at : at + 5]
    copies = [
        pltpu.make_async_copy(kv_refs[shard], held.at[shard], sems.at[shard])
        for shard in range(shards)
    ]
    for copy in copies:
        copy.start()
    token[...] = jnp.zeros(token.shape, jnp.float32)
    if resume:
        peak[...] = peak_in[...]
        sums[...] = sums_in[...]
    else:
        peak[...] = jnp.full(peak.shape, NEGATIVE, jnp.float32)
        sums[...] = jnp.zeros(sums.shape, jnp.float32)

    def one_block(shard, base, length, high):
        key = held[shard, pl.ds(base, high), :HD]
        value = held[shard, pl.ds(base, high), HD:]
        valid = base + lax.broadcasted_iota(jnp.int32, (high, HD), 0) < length
        first = held[shard, 0:16, :HD].astype(jnp.float32)[0:1]
        key = jnp.where(valid, key.astype(jnp.float32), first).astype(jnp.bfloat16)
        value = jnp.where(valid, value.astype(jnp.float32), 0.0).astype(jnp.bfloat16)
        ones = jnp.where(valid, 1.0, 0.0).astype(jnp.bfloat16)
        value = jnp.concatenate([value, ones], axis=1)

        def score(unit):
            return lax.dot_general(
                q_ref[:, unit * HD : (unit + 1) * HD],
                key,
                (((1,), (1,)), ((), ())),
                preferred_element_type=jnp.float32,
            )

        following = score(0)
        for unit in range(units):
            scores = following
            if unit + 1 < units:
                following = score(unit + 1)
            before = peak[unit]
            top = jnp.maximum(before, jnp.max(scores, axis=1, keepdims=True))
            peak[unit] = top
            probs = jnp.exp2(
                (scores - jnp.concatenate([top] * (high // HD), axis=1)) * SCALE_LOG2
            ).astype(jnp.bfloat16)
            fade = jnp.exp2((before - top) * SCALE_LOG2)
            sums[unit] = sums[unit] * jnp.concatenate([fade, fade], axis=1) + jnp.dot(
                probs, value, preferred_element_type=jnp.float32
            )

    context = held.shape[1] - MARKS

    @pl.loop(0, shards)
    def _(shard):
        for at, copy in enumerate(copies):

            @pl.when(shard == at)
            def _(copy=copy):
                copy.wait()

        marks = jnp.max(
            held[shard, context : context + MARKS, :HD]
            .astype(jnp.float32)
            .reshape(2, MARKS // 2, HD),
            axis=1,
        ).astype(jnp.int32)
        length = jnp.max(marks[0:1]) * 256 + jnp.max(marks[1:2])
        small = block // 2
        whole = (length + small - 1) // block

        @pl.loop(0, whole)
        def _(step):
            one_block(shard, pl.multiple_of(step * block, block), length, block)

        @pl.when(whole * block < length)
        def _():
            one_block(shard, pl.multiple_of(whole * block, block), length, small)

    if finish:
        for unit in range(units):
            total = sums[unit]
            out_ref[:, unit * HD : (unit + 1) * HD] = (total[:, :HD] / total[:, HD:]).astype(
                jnp.bfloat16
            )


def attend(query, caches, state=None, finish=False, behind=None):
    rows, width = query.shape
    units = width // HD
    shards = len(caches)
    peak = jax.ShapeDtypeStruct((units, rows, HD), jnp.float32)
    sums = jax.ShapeDtypeStruct((units, rows, 2 * HD), jnp.float32)
    vmem = pl.BlockSpec(memory_space=pltpu.VMEM)
    operands = [query, *caches]
    if state is not None:
        operands += list(state)
    if finish:
        out_shape = (jax.ShapeDtypeStruct(query.shape, jnp.bfloat16), TOKEN)
        scratch = [pltpu.VMEM(peak.shape, peak.dtype), pltpu.VMEM(sums.shape, sums.dtype)]
    else:
        out_shape = (peak, sums, TOKEN)
        scratch = []
    in_specs = [vmem] * len(operands)
    in_specs[1 : 1 + shards] = [pl.BlockSpec(memory_space=pltpu.HBM)] * shards
    scratch += [
        pltpu.VMEM((shards, *caches[0].shape), jnp.bfloat16),
        pltpu.SemaphoreType.DMA((shards,)),
    ]
    if behind is not None:
        operands.append(behind)
        in_specs.append(pl.BlockSpec(memory_space=pl.ANY))
    return pl.pallas_call(
        functools.partial(
            attend_body,
            shards=shards,
            units=units,
            resume=state is not None,
            finish=finish,
            ordered=behind is not None,
            block=KEY_BLOCK,
        ),
        out_shape=out_shape,
        in_specs=in_specs,
        out_specs=(vmem,) * len(out_shape),
        scratch_shapes=scratch,
        compiler_params=pltpu.CompilerParams(vmem_limit_bytes=SMALL_VMEM),
        cost_estimate=LIGHT,
    )(*operands)


def swap_pairs(size, mask):
    return [(index, index ^ mask) for index in range(size)]


def add(one, two):
    return (one.astype(jnp.float32) + two.astype(jnp.float32)).astype(jnp.bfloat16)


def split_projection(query, keys, values, cache_lengths, out_weight):
    size = lax.axis_size("aa")
    index = lax.axis_index("aa")
    side = index // 2
    over = functools.partial(lax.ppermute, axis_name="aa", perm=swap_pairs(size, 2))
    core = functools.partial(lax.ppermute, axis_name="aa", perm=swap_pairs(size, 1))
    half = query.shape[1] // 2

    own_query, away_query, own_cache, away_cache = prepare(
        side, cache_lengths, query, keys, values
    )
    far_query = over(away_query)
    far_cache = over(away_cache)
    near_cache = core(own_cache)
    *own_state, token = attend(own_query, [own_cache, near_cache])
    far_cache = after(far_cache, token)
    corner_cache = core(far_cache)
    own_rows, token = attend(own_query, [far_cache, corner_cache], own_state, True)
    far_other = over(own_rows)
    *far_state, token = attend(far_query, [own_cache, near_cache], behind=token)
    far_rows, token = attend(
        far_query, [far_cache, corner_cache], far_state, True, behind=far_other
    )
    own_other = over(far_rows)
    first = jnp.stack([own_rows, far_rows, core(own_rows), core(far_rows)])
    second = jnp.stack([own_other, far_other, core(own_other), core(far_other)])
    first_weight = lax.dynamic_slice_in_dim(out_weight, side * half, half, 0)
    second_weight = lax.dynamic_slice_in_dim(out_weight, (1 - side) * half, half, 0)

    place = lax.axis_index("ba")
    low = place < 2
    order = (jnp.where(low, 3, 0), jnp.where(low, 2, 1), place ^ 1, place)
    columns = out_weight.shape[1]
    cut = columns // 2 if columns % (2 * HD) == 0 else columns

    def product(step, begin):
        mask = index ^ order[step]
        slot = mask // 2 + 2 * (mask % 2)
        left = lax.dynamic_index_in_dim(first, slot, 0, False)
        right = lax.dynamic_index_in_dim(second, slot, 0, False)
        return jnp.dot(
            left, first_weight[:, begin : begin + cut], preferred_element_type=jnp.float32
        ) + jnp.dot(
            right, second_weight[:, begin : begin + cut], preferred_element_type=jnp.float32
        )

    send = functools.partial(lax.ppermute, axis_name="ba")
    starts = range(0, columns, cut)
    one = [product(0, begin).astype(jnp.bfloat16) for begin in starts]
    up = [send(part, perm=[(0, 1), (3, 2)]) for part in one]
    down = list(up)
    two = [product(1, begin).astype(jnp.bfloat16) for begin in starts]
    for at in range(len(one)):
        up[at] = send(
            add(jnp.where(place == 0, two[at], one[at]), up[at]), perm=[(0, 1), (1, 2)]
        )
        down[at] = send(
            add(jnp.where(place == 3, two[at], one[at]), down[at]), perm=[(3, 2), (2, 1)]
        )
    three = [product(2, begin).astype(jnp.bfloat16) for begin in starts]
    for at in range(len(one)):
        up[at] = send(
            add(jnp.where(place == 1, two[at], three[at]), up[at]),
            perm=[(0, 1), (1, 2), (2, 3)],
        )
        down[at] = send(
            add(jnp.where(place == 2, two[at], three[at]), down[at]),
            perm=[(3, 2), (2, 1), (1, 0)],
        )
    return jnp.concatenate(
        [
            product(3, begin) + up[at].astype(jnp.float32) + down[at].astype(jnp.float32)
            for at, begin in enumerate(starts)
        ],
        axis=1,
    )


def expert_body(quarter, *refs, blocks, ordered, tile):
    piece_refs = refs[: 4 * blocks]
    gate_hbm, up_hbm, down_hbm = refs[4 * blocks : 4 * blocks + 3]
    out_ref, token, gate_w, up_w, down_w, gate_sum, up_sum, act, sems = refs[
        4 * blocks + 3 + ordered :
    ]
    _, width, hidden_units = gate_w.shape
    inward, outward = [], []
    for piece in range(4):
        at = pl.ds(pl.multiple_of(quarter[piece] * width, HD), width)
        inward.append(
            [
                pltpu.make_async_copy(gate_hbm.at[0, at, :], gate_w.at[piece], sems.at[0, piece]),
                pltpu.make_async_copy(up_hbm.at[0, at, :], up_w.at[piece], sems.at[1, piece]),
            ]
        )
        outward.append(
            pltpu.make_async_copy(down_hbm.at[0, :, at], down_w.at[piece], sems.at[2, piece])
        )
    for pair in inward:
        for copy in pair:
            copy.start()
    for copy in outward:
        copy.start()
    token[...] = jnp.zeros(token.shape, jnp.float32)
    factors = []
    for block in range(blocks):
        total = 0.0
        for piece in range(4):
            total += jnp.sum(
                piece_refs[4 * block + piece][:, width:].astype(jnp.float32), axis=1, keepdims=True
            )
        factors.append(1.0 / jnp.sqrt(total / (4 * width) + EPSILON))
    scale = jnp.concatenate(factors, axis=0)
    for piece in range(4):
        operand = jnp.concatenate(
            [piece_refs[4 * block + piece][:, :width] for block in range(blocks)], axis=0
        )
        for copy, weight, total in zip(inward[piece], (gate_w, up_w), (gate_sum, up_sum)):
            copy.wait()
            for begin in range(0, hidden_units, tile):
                columns = slice(begin, begin + tile)
                part = jnp.dot(
                    operand, weight[piece, :, columns], preferred_element_type=jnp.float32
                )
                if piece > 0:
                    part += total[:, columns]
                total[:, columns] = part
    for begin in range(0, hidden_units, tile):
        columns = slice(begin, begin + tile)
        gate_part = gate_sum[:, columns] * scale
        act[:, columns] = (
            gate_part / (1.0 + jnp.exp(-gate_part)) * (up_sum[:, columns] * scale)
        ).astype(jnp.bfloat16)
    for piece in range(4):
        outward[piece].wait()
        for begin in range(0, width, tile):
            columns = slice(begin, begin + tile)
            out_ref[piece, :, columns] = jnp.dot(
                act[...], down_w[piece, :, columns], preferred_element_type=jnp.float32
            ).astype(jnp.bfloat16)


def expert_call(quarter, pieces, gate_w, up_w, down_w, behind=None):
    blocks = len(pieces)
    rows = pieces[0][0].shape[0]
    width = gate_w.shape[1] // 4
    hidden_units = gate_w.shape[2]
    high = blocks * rows
    vmem = pl.BlockSpec(memory_space=pltpu.VMEM)
    flat = [piece for block in pieces for piece in block]
    operands = [quarter, *flat, gate_w, up_w, down_w]
    in_specs = [pl.BlockSpec(memory_space=pltpu.SMEM)] + [vmem] * len(flat)
    in_specs += [pl.BlockSpec(memory_space=pltpu.HBM)] * 3
    if behind is not None:
        operands.append(behind)
        in_specs.append(pl.BlockSpec(memory_space=pl.ANY))
    return pl.pallas_call(
        functools.partial(expert_body, blocks=blocks, ordered=behind is not None, tile=2 * HD),
        in_specs=in_specs,
        out_specs=(vmem, vmem),
        out_shape=(jax.ShapeDtypeStruct((4, high, width), jnp.bfloat16), TOKEN),
        scratch_shapes=[
            pltpu.VMEM((4, width, hidden_units), jnp.bfloat16),
            pltpu.VMEM((4, width, hidden_units), jnp.bfloat16),
            pltpu.VMEM((4, hidden_units, width), jnp.bfloat16),
            pltpu.VMEM((high, hidden_units), jnp.float32),
            pltpu.VMEM((high, hidden_units), jnp.float32),
            pltpu.VMEM((high, hidden_units), jnp.bfloat16),
            pltpu.SemaphoreType.DMA((3, 4)),
        ],
        compiler_params=pltpu.CompilerParams(vmem_limit_bytes=EXPERT_VMEM),
        cost_estimate=LIGHT,
    )(*operands)


def routed_experts(
    gained, squares, stats, expert_ids, expert_slots, slot_count, gate_w, up_w, down_w
):
    size = lax.axis_size("aa")
    index = lax.axis_index("aa")
    depth = lax.axis_size("ba")
    place = lax.axis_index("ba")
    over = functools.partial(lax.ppermute, axis_name="aa", perm=swap_pairs(size, 2))
    core = functools.partial(lax.ppermute, axis_name="aa", perm=swap_pairs(size, 1))

    def shift(array, by):
        return lax.ppermute(
            array, "ba", perm=[(at, (at + by) % depth) for at in range(depth)]
        )

    ahead = lax.rem(expert_ids - place + depth, depth)
    combined = ahead * slot_count + expert_slots
    chosen = (
        combined[:, None] == lax.broadcasted_iota(jnp.int32, (1, depth * slot_count), 1)
    ) & (expert_slots[:, None] >= 0)
    placing = chosen.astype(jnp.bfloat16)
    coarse = squares.astype(jnp.bfloat16)
    fine = (squares - coarse.astype(jnp.float32)).astype(jnp.bfloat16)
    rows = jnp.concatenate(
        [
            gained.astype(jnp.bfloat16),
            coarse,
            fine,
            jnp.zeros((gained.shape[0], HD - 2), jnp.bfloat16),
        ],
        axis=1,
    )
    slots = [slice(at * slot_count, (at + 1) * slot_count) for at in range(depth)]
    parts = [
        lax.dot_general(
            placing[:, slots[at]], rows, (((0,), (0,)), ((), ())), preferred_element_type=jnp.float32
        ).astype(jnp.bfloat16)
        for at in range(depth)
    ]

    def widen(block, far=None):
        far = over(block) if far is None else far
        both = core(jnp.stack([block, far]))
        return [block, far, both[0], both[1]]

    arrived = [parts[0], shift(parts[1], 1), None, shift(parts[3], 3)]
    arrived[2] = shift(parts[2], 2)
    quarter = jnp.stack([index, index ^ 2, index ^ 1, index ^ 3]).astype(jnp.int32)

    def narrow(share):
        return add(share[:2], core(share[2:]))

    weights = (gate_w, up_w, down_w)
    one, token = expert_call(quarter, [widen(arrived[0]), widen(arrived[1])], *weights)
    stats = after(stats.T, token)
    stats = stats + core(stats)
    stats = (stats + over(stats)).T
    one = narrow(one)
    low, high = slice(0, slot_count), slice(slot_count, 2 * slot_count)
    third = widen(arrived[3], after(over(arrived[3]), token))
    second = widen(after(arrived[2], token))
    two, token = expert_call(quarter, [third, second], *weights, stats)
    two = narrow(two)
    back = [None] * depth
    crossed = over(two[1, high])
    back[2] = shift(add(two[0, high], crossed), -2)
    back[3] = shift(add(two[0, low], over(two[1, low])), -3)
    near = over(after(one, crossed)[1, high])
    back[1] = shift(add(one[0, high], near), -1)
    back[0] = add(one[0, low], over(after(one, near)[1, low]))
    return lax.dot_general(
        placing,
        jnp.concatenate(back, axis=0),
        (((1,), (0,)), ((), ())),
        preferred_element_type=jnp.float32,
    ), stats


def gathered_experts(
    gained, squares, stats, expert_ids, expert_slots, slot_count, gate_w, up_w, down_w
):
    stats = lax.psum(stats, "aa")
    width = gained.shape[1] * lax.axis_size("aa")
    inverse = 1.0 / jnp.sqrt(stats[:, :1] / width + EPSILON)
    expert_in = (gained * inverse).astype(jnp.bfloat16)
    experts = gate_w.shape[0] * lax.axis_size("ba")
    combined = expert_ids * slot_count + expert_slots
    placing = (
        combined[:, None] == lax.broadcasted_iota(jnp.int32, (1, experts * slot_count), 1)
    ) & (expert_slots[:, None] >= 0)
    placing = placing.astype(jnp.bfloat16)
    packed = lax.dot_general(
        placing, expert_in, (((0,), (0,)), ((), ())), preferred_element_type=jnp.float32
    ).astype(jnp.bfloat16)
    arrived = lax.all_to_all(packed, "ba", split_axis=0, concat_axis=0, tiled=True)
    piece = lax.all_gather(arrived, "aa", axis=1, tiled=True)
    gate_part = jnp.dot(piece, gate_w[0], preferred_element_type=jnp.float32)
    up_part = jnp.dot(piece, up_w[0], preferred_element_type=jnp.float32)
    act = (jax.nn.silu(gate_part) * up_part).astype(jnp.bfloat16)
    expert_out = lax.psum_scatter(
        lax.dot_general(
            down_w[0], act, (((0,), (1,)), ((), ())), preferred_element_type=jnp.float32
        ).astype(jnp.bfloat16),
        "aa",
        scatter_dimension=0,
        tiled=True,
    )
    returned = lax.all_to_all(expert_out, "ba", split_axis=1, concat_axis=1, tiled=True)
    return lax.dot_general(
        placing, returned, (((1,), (1,)), ((), ())), preferred_element_type=jnp.float32
    ), stats


def on_device(
    query,
    keys,
    values,
    cache_lengths,
    residual,
    out_weight,
    norm_gain,
    router_weight,
    expert_ids,
    expert_slots,
    expert_gate,
    expert_up,
    expert_down,
):
    square = lax.axis_size("aa") == 4 and lax.axis_size("ba") == 4
    split = (
        square
        and keys.shape[1] == 2 * HD
        and keys.shape[0] % KEY_BLOCK == 0
        and query.shape[0] == residual.shape[0]
    )
    project = split_projection if split else plain_projection
    hidden = residual.astype(jnp.float32) + project(
        query, keys, values, cache_lengths, out_weight
    )
    width = hidden.shape[1] * lax.axis_size("aa")
    experts = router_weight.shape[1]
    gained = hidden * norm_gain
    squares = jnp.sum(hidden * hidden, axis=1, keepdims=True)
    raw = jnp.dot(gained, router_weight, precision=lax.Precision.HIGHEST)
    stats = jnp.concatenate([squares, raw], axis=1)

    slot_count = 2 * query.shape[0] * lax.axis_size("aa") // (lax.axis_size("ba") * experts)
    run = routed_experts if square and expert_gate.shape[0] == 1 else gathered_experts
    from_experts, sums = run(
        gained,
        squares,
        stats,
        expert_ids,
        expert_slots,
        slot_count,
        expert_gate,
        expert_up,
        expert_down,
    )
    logits = sums[:, 1:] / jnp.sqrt(sums[:, :1] / width + EPSILON)
    chosen = expert_ids[:, None] == lax.broadcasted_iota(jnp.int32, (1, experts), 1)
    gate = jnp.sum(jnp.where(chosen, jax.nn.sigmoid(logits), 0.0), axis=1)
    return (hidden + gate[:, None] * from_experts).astype(jnp.bfloat16)


def solution(mesh):
    return jax.shard_map(
        on_device,
        mesh=mesh,
        in_specs=(
            P(("ga", "aa"), "ba"),
            P(("ga", "aa"), "ba"),
            P(("ga", "aa"), "ba"),
            P(("ga", "aa")),
            P(("ga", "ba"), "aa"),
            P("ba", "aa"),
            P("aa"),
            P("aa", None),
            P(("ga", "ba")),
            P(("ga", "ba")),
            P("ba", None, "aa"),
            P("ba", None, "aa"),
            P("ba", "aa", None),
        ),
        out_specs=P(("ga", "ba"), "aa"),
        check_vma=False,
    )
```

```python
import functools
import math

import jax
import jax.numpy as jnp
from jax import lax
from jax.experimental import pallas as pl
from jax.experimental.pallas import tpu as pltpu
from jax.sharding import PartitionSpec as P

HD = 128
KEY_BLOCK = 1024
MARKS = 32
SMALL_VMEM = 16 * 1024 * 1024
EXPERT_VMEM = 52 * 1024 * 1024
LARGE_VMEM = 62 * 1024 * 1024 - 512 * 1024
TOKEN = jax.ShapeDtypeStruct((8, HD), jnp.float32)
LIGHT = pl.CostEstimate(flops=1000, bytes_accessed=1000, transcendentals=0)
NEGATIVE = -1e30
EPSILON = 1e-05
SCALE = HD ** (-0.5)
SCALE_LOG2 = SCALE * math.log2(math.e)


def head_partials(rows, key_block, value_block, length):
    heads = rows.shape[1] // HD
    kv_heads = key_block.shape[1] // HD
    group = heads // kv_heads
    valid = lax.broadcasted_iota(jnp.int32, (1, key_block.shape[0]), 1) < length
    maxima = []
    totals = []
    outputs = []
    for head in range(heads):
        source = head // group
        q_head = rows[:, head * HD : (head + 1) * HD]
        k_head = key_block[:, source * HD : (source + 1) * HD]
        v_head = value_block[:, source * HD : (source + 1) * HD]
        scores = lax.dot_general(
            q_head, k_head, (((1,), (1,)), ((), ())), preferred_element_type=jnp.float32
        ) * SCALE
        scores = jnp.where(valid, scores, NEGATIVE)
        peak = jnp.max(scores, axis=1)
        probs = jnp.exp(scores - peak[:, None])
        maxima.append(peak)
        totals.append(jnp.sum(probs, axis=1))
        outputs.append(
            jnp.dot(probs.astype(jnp.bfloat16), v_head, preferred_element_type=jnp.float32)
        )
    return (jnp.stack(maxima, axis=1), jnp.stack(totals, axis=1), jnp.concatenate(outputs, axis=1))


def combine_partials(first, second):
    peak_one, total_one, out_one = first
    peak_two, total_two, out_two = second
    peak = jnp.maximum(peak_one, peak_two)
    scale_one = jnp.exp(peak_one - peak)
    scale_two = jnp.exp(peak_two - peak)
    outputs = out_one * jnp.repeat(scale_one, HD, axis=1) + out_two * jnp.repeat(
        scale_two, HD, axis=1
    )
    return (peak, total_one * scale_one + total_two * scale_two, outputs)


def plain_projection(query, keys, values, cache_lengths, out_weight):
    heads = query.shape[1] // HD
    own_rows = query.shape[0]
    context = keys.shape[0]
    start_state = (
        jnp.full((own_rows, heads), NEGATIVE, jnp.float32),
        jnp.zeros((own_rows, heads), jnp.float32),
        jnp.zeros((own_rows, heads * HD), jnp.float32),
    )
    key_piece = lax.all_gather(keys, "aa", axis=0, tiled=True)
    value_piece = lax.all_gather(values, "aa", axis=0, tiled=True)
    length_piece = lax.all_gather(cache_lengths, "aa", axis=0, tiled=True)

    def one_shard(index, carry):
        key_block = lax.dynamic_slice_in_dim(key_piece, index * context, context, 0)
        value_block = lax.dynamic_slice_in_dim(value_piece, index * context, context, 0)
        return combine_partials(
            carry, head_partials(query, key_block, value_block, length_piece[index])
        )

    peak, total, weighted = lax.fori_loop(0, length_piece.shape[0], one_shard, start_state)
    own = (weighted / jnp.repeat(total, HD, axis=1)).astype(jnp.bfloat16)
    attended = lax.all_gather(own, "aa", axis=0, tiled=True)
    return lax.psum_scatter(
        jnp.dot(attended, out_weight, preferred_element_type=jnp.float32).astype(jnp.bfloat16),
        "ba",
        scatter_dimension=0,
        tiled=True,
    ).astype(jnp.float32)


def prepare_body(scalars, q_ref, k_ref, v_ref, own_query, far_query, own_cache, far_cache, marks, sems):
    side, length = scalars[0], scalars[1]
    context = k_ref.shape[0]
    half = own_query.shape[1]
    rows = MARKS // 2
    marks[:rows] = jnp.full((rows, 2 * HD), length // 256, jnp.int32).astype(jnp.float32).astype(jnp.bfloat16)
    marks[rows:] = jnp.full((rows, 2 * HD), lax.rem(length, 256), jnp.int32).astype(jnp.float32).astype(jnp.bfloat16)
    copies = []
    for query_out, cache_out, which in (
        (far_query, far_cache, 1 - side),
        (own_query, own_cache, side),
    ):
        column = pl.ds(pl.multiple_of(which * HD, HD), HD)
        for source, target in (
            (q_ref.at[:, pl.ds(pl.multiple_of(which * half, HD), half)], query_out),
            (k_ref.at[:, column], cache_out.at[pl.ds(0, context), pl.ds(0, HD)]),
            (v_ref.at[:, column], cache_out.at[pl.ds(0, context), pl.ds(HD, HD)]),
            (marks, cache_out.at[pl.ds(context, MARKS), :]),
        ):
            copy = pltpu.make_async_copy(source, target, sems.at[len(copies)])
            copy.start()
            copies.append(copy)
    for copy in copies:
        copy.wait()


def prepare(side, cache_lengths, query, keys, values):
    scalars = jnp.concatenate([side[None].astype(jnp.int32), cache_lengths])
    hbm = pl.BlockSpec(memory_space=pltpu.HBM)
    half = jax.ShapeDtypeStruct((query.shape[0], query.shape[1] // 2), jnp.bfloat16)
    cache = jax.ShapeDtypeStruct((keys.shape[0] + MARKS, 2 * HD), jnp.bfloat16)
    return pl.pallas_call(
        prepare_body,
        out_shape=(half, half, cache, cache),
        in_specs=[pl.BlockSpec(memory_space=pltpu.SMEM), hbm, hbm, hbm],
        out_specs=(hbm, hbm, hbm, hbm),
        scratch_shapes=[
            pltpu.VMEM((MARKS, 2 * HD), jnp.bfloat16),
            pltpu.SemaphoreType.DMA((8,)),
        ],
        compiler_params=pltpu.CompilerParams(vmem_limit_bytes=LARGE_VMEM),
    )(scalars, query, keys, values)


def after_body(*refs):
    pass


def after(value, *others):
    anywhere = pl.BlockSpec(memory_space=pl.ANY)
    return pl.pallas_call(
        after_body,
        out_shape=jax.ShapeDtypeStruct(value.shape, value.dtype),
        in_specs=[anywhere] * (1 + len(others)),
        out_specs=anywhere,
        input_output_aliases={0: 0},
        compiler_params=pltpu.CompilerParams(vmem_limit_bytes=SMALL_VMEM),
        cost_estimate=LIGHT,
    )(value, *others)


def attend_body(*refs, shards, units, resume, finish, ordered, block):
    q_ref = refs[0]
    kv_refs = refs[1 : 1 + shards]
    at = 1 + shards
    if resume:
        peak_in, sums_in = refs[at : at + 2]
        at += 2
    at += ordered
    if finish:
        out_ref, token, peak, sums, held, sems = refs[at : at + 6]
    else:
        peak, sums, token, held, sems = refs[at : at + 5]
    copies = [
        pltpu.make_async_copy(kv_refs[shard], held.at[shard], sems.at[shard])
        for shard in range(shards)
    ]
    for copy in copies:
        copy.start()
    token[...] = jnp.zeros(token.shape, jnp.float32)
    if resume:
        peak[...] = peak_in[...]
        sums[...] = sums_in[...]
    else:
        peak[...] = jnp.full(peak.shape, NEGATIVE, jnp.float32)
        sums[...] = jnp.zeros(sums.shape, jnp.float32)

    def one_block(shard, base, length, high):
        key = held[shard, pl.ds(base, high), :HD]
        value = held[shard, pl.ds(base, high), HD:]
        valid = base + lax.broadcasted_iota(jnp.int32, (high, HD), 0) < length
        first = held[shard, 0:16, :HD].astype(jnp.float32)[0:1]
        key = jnp.where(valid, key.astype(jnp.float32), first).astype(jnp.bfloat16)
        value = jnp.where(valid, value.astype(jnp.float32), 0.0).astype(jnp.bfloat16)
        ones = jnp.where(valid, 1.0, 0.0).astype(jnp.bfloat16)
        value = jnp.concatenate([value, ones], axis=1)

        def score(unit):
            return lax.dot_general(
                q_ref[:, unit * HD : (unit + 1) * HD],
                key,
                (((1,), (1,)), ((), ())),
                preferred_element_type=jnp.float32,
            )

        following = score(0)
        for unit in range(units):
            scores = following
            if unit + 1 < units:
                following = score(unit + 1)
            before = peak[unit]
            top = jnp.maximum(before, jnp.max(scores, axis=1, keepdims=True))
            peak[unit] = top
            probs = jnp.exp2(
                (scores - jnp.concatenate([top] * (high // HD), axis=1)) * SCALE_LOG2
            ).astype(jnp.bfloat16)
            fade = jnp.exp2((before - top) * SCALE_LOG2)
            sums[unit] = sums[unit] * jnp.concatenate([fade, fade], axis=1) + jnp.dot(
                probs, value, preferred_element_type=jnp.float32
            )

    context = held.shape[1] - MARKS

    @pl.loop(0, shards)
    def _(shard):
        for at, copy in enumerate(copies):

            @pl.when(shard == at)
            def _(copy=copy):
                copy.wait()

        marks = jnp.max(
            held[shard, context : context + MARKS, :HD]
            .astype(jnp.float32)
            .reshape(2, MARKS // 2, HD),
            axis=1,
        ).astype(jnp.int32)
        length = jnp.max(marks[0:1]) * 256 + jnp.max(marks[1:2])
        small = block // 2
        whole = (length + small - 1) // block

        @pl.loop(0, whole)
        def _(step):
            one_block(shard, pl.multiple_of(step * block, block), length, block)

        @pl.when(whole * block < length)
        def _():
            one_block(shard, pl.multiple_of(whole * block, block), length, small)

    if finish:
        for unit in range(units):
            total = sums[unit]
            out_ref[:, unit * HD : (unit + 1) * HD] = (total[:, :HD] / total[:, HD:]).astype(
                jnp.bfloat16
            )


def attend(query, caches, state=None, finish=False, behind=None):
    rows, width = query.shape
    units = width // HD
    shards = len(caches)
    peak = jax.ShapeDtypeStruct((units, rows, HD), jnp.float32)
    sums = jax.ShapeDtypeStruct((units, rows, 2 * HD), jnp.float32)
    vmem = pl.BlockSpec(memory_space=pltpu.VMEM)
    operands = [query, *caches]
    if state is not None:
        operands += list(state)
    if finish:
        out_shape = (jax.ShapeDtypeStruct(query.shape, jnp.bfloat16), TOKEN)
        scratch = [pltpu.VMEM(peak.shape, peak.dtype), pltpu.VMEM(sums.shape, sums.dtype)]
    else:
        out_shape = (peak, sums, TOKEN)
        scratch = []
    in_specs = [vmem] * len(operands)
    in_specs[1 : 1 + shards] = [pl.BlockSpec(memory_space=pltpu.HBM)] * shards
    scratch += [
        pltpu.VMEM((shards, *caches[0].shape), jnp.bfloat16),
        pltpu.SemaphoreType.DMA((shards,)),
    ]
    if behind is not None:
        operands.append(behind)
        in_specs.append(pl.BlockSpec(memory_space=pl.ANY))
    return pl.pallas_call(
        functools.partial(
            attend_body,
            shards=shards,
            units=units,
            resume=state is not None,
            finish=finish,
            ordered=behind is not None,
            block=KEY_BLOCK,
        ),
        out_shape=out_shape,
        in_specs=in_specs,
        out_specs=(vmem,) * len(out_shape),
        scratch_shapes=scratch,
        compiler_params=pltpu.CompilerParams(vmem_limit_bytes=SMALL_VMEM),
        cost_estimate=LIGHT,
    )(*operands)


def swap_pairs(size, mask):
    return [(index, index ^ mask) for index in range(size)]


def add(one, two):
    return (one.astype(jnp.float32) + two.astype(jnp.float32)).astype(jnp.bfloat16)


def split_projection(query, keys, values, cache_lengths, out_weight):
    size = lax.axis_size("aa")
    index = lax.axis_index("aa")
    side = index // 2
    over = functools.partial(lax.ppermute, axis_name="aa", perm=swap_pairs(size, 2))
    core = functools.partial(lax.ppermute, axis_name="aa", perm=swap_pairs(size, 1))
    half = query.shape[1] // 2

    own_query, away_query, own_cache, away_cache = prepare(
        side, cache_lengths, query, keys, values
    )
    far_query = over(away_query)
    far_cache = over(away_cache)
    near_cache = core(own_cache)
    *own_state, token = attend(own_query, [own_cache, near_cache])
    far_cache = after(far_cache, token)
    corner_cache = core(far_cache)
    own_rows, token = attend(own_query, [far_cache, corner_cache], own_state, True)
    far_other = over(own_rows)
    *far_state, token = attend(far_query, [own_cache, near_cache], behind=token)
    far_rows, token = attend(
        far_query, [far_cache, corner_cache], far_state, True, behind=far_other
    )
    own_other = over(far_rows)
    first = jnp.stack([own_rows, far_rows, core(own_rows), core(far_rows)])
    second = jnp.stack([own_other, far_other, core(own_other), core(far_other)])
    first_weight = lax.dynamic_slice_in_dim(out_weight, side * half, half, 0)
    second_weight = lax.dynamic_slice_in_dim(out_weight, (1 - side) * half, half, 0)

    place = lax.axis_index("ba")
    low = place < 2
    order = (jnp.where(low, 3, 0), jnp.where(low, 2, 1), place ^ 1, place)
    columns = out_weight.shape[1]
    cut = columns // 2 if columns % (2 * HD) == 0 else columns

    def product(step, begin):
        mask = index ^ order[step]
        slot = mask // 2 + 2 * (mask % 2)
        left = lax.dynamic_index_in_dim(first, slot, 0, False)
        right = lax.dynamic_index_in_dim(second, slot, 0, False)
        return jnp.dot(
            left, first_weight[:, begin : begin + cut], preferred_element_type=jnp.float32
        ) + jnp.dot(
            right, second_weight[:, begin : begin + cut], preferred_element_type=jnp.float32
        )

    send = functools.partial(lax.ppermute, axis_name="ba")
    starts = range(0, columns, cut)
    one = [product(0, begin).astype(jnp.bfloat16) for begin in starts]
    up = [send(part, perm=[(0, 1), (3, 2)]) for part in one]
    down = list(up)
    two = [product(1, begin).astype(jnp.bfloat16) for begin in starts]
    for at in range(len(one)):
        up[at] = send(
            add(jnp.where(place == 0, two[at], one[at]), up[at]), perm=[(0, 1), (1, 2)]
        )
        down[at] = send(
            add(jnp.where(place == 3, two[at], one[at]), down[at]), perm=[(3, 2), (2, 1)]
        )
    three = [product(2, begin).astype(jnp.bfloat16) for begin in starts]
    for at in range(len(one)):
        up[at] = send(
            add(jnp.where(place == 1, two[at], three[at]), up[at]),
            perm=[(0, 1), (1, 2), (2, 3)],
        )
        down[at] = send(
            add(jnp.where(place == 2, two[at], three[at]), down[at]),
            perm=[(3, 2), (2, 1), (1, 0)],
        )
    return jnp.concatenate(
        [
            product(3, begin) + up[at].astype(jnp.float32) + down[at].astype(jnp.float32)
            for at, begin in enumerate(starts)
        ],
        axis=1,
    )


def expert_body(quarter, *refs, blocks, ordered, tile):
    piece_refs = refs[: 4 * blocks]
    gate_hbm, up_hbm, down_hbm = refs[4 * blocks : 4 * blocks + 3]
    out_ref, token, gate_w, up_w, down_w, gate_sum, up_sum, act, sems = refs[
        4 * blocks + 3 + ordered :
    ]
    _, width, hidden_units = gate_w.shape
    inward, outward = [], []
    for piece in range(4):
        at = pl.ds(pl.multiple_of(quarter[piece] * width, HD), width)
        inward.append(
            [
                pltpu.make_async_copy(gate_hbm.at[0, at, :], gate_w.at[piece], sems.at[0, piece]),
                pltpu.make_async_copy(up_hbm.at[0, at, :], up_w.at[piece], sems.at[1, piece]),
            ]
        )
        outward.append(
            pltpu.make_async_copy(down_hbm.at[0, :, at], down_w.at[piece], sems.at[2, piece])
        )
    for pair in inward:
        for copy in pair:
            copy.start()
    for copy in outward:
        copy.start()
    token[...] = jnp.zeros(token.shape, jnp.float32)
    factors = []
    for block in range(blocks):
        total = 0.0
        for piece in range(4):
            total += jnp.sum(
                piece_refs[4 * block + piece][:, width:].astype(jnp.float32), axis=1, keepdims=True
            )
        factors.append(1.0 / jnp.sqrt(total / (4 * width) + EPSILON))
    scale = jnp.concatenate(factors, axis=0)
    for piece in range(4):
        operand = jnp.concatenate(
            [piece_refs[4 * block + piece][:, :width] for block in range(blocks)], axis=0
        )
        for copy, weight, total in zip(inward[piece], (gate_w, up_w), (gate_sum, up_sum)):
            copy.wait()
            for begin in range(0, hidden_units, tile):
                columns = slice(begin, begin + tile)
                part = jnp.dot(
                    operand, weight[piece, :, columns], preferred_element_type=jnp.float32
                )
                if piece > 0:
                    part += total[:, columns]
                total[:, columns] = part
    for begin in range(0, hidden_units, tile):
        columns = slice(begin, begin + tile)
        gate_part = gate_sum[:, columns] * scale
        act[:, columns] = (
            gate_part / (1.0 + jnp.exp(-gate_part)) * (up_sum[:, columns] * scale)
        ).astype(jnp.bfloat16)
    for piece in range(4):
        outward[piece].wait()
        for begin in range(0, width, tile):
            columns = slice(begin, begin + tile)
            out_ref[piece, :, columns] = jnp.dot(
                act[...], down_w[piece, :, columns], preferred_element_type=jnp.float32
            ).astype(jnp.bfloat16)


def expert_call(quarter, pieces, gate_w, up_w, down_w, behind=None):
    blocks = len(pieces)
    rows = pieces[0][0].shape[0]
    width = gate_w.shape[1] // 4
    hidden_units = gate_w.shape[2]
    high = blocks * rows
    vmem = pl.BlockSpec(memory_space=pltpu.VMEM)
    flat = [piece for block in pieces for piece in block]
    operands = [quarter, *flat, gate_w, up_w, down_w]
    in_specs = [pl.BlockSpec(memory_space=pltpu.SMEM)] + [vmem] * len(flat)
    in_specs += [pl.BlockSpec(memory_space=pltpu.HBM)] * 3
    if behind is not None:
        operands.append(behind)
        in_specs.append(pl.BlockSpec(memory_space=pl.ANY))
    return pl.pallas_call(
        functools.partial(expert_body, blocks=blocks, ordered=behind is not None, tile=2 * HD),
        in_specs=in_specs,
        out_specs=(vmem, vmem),
        out_shape=(jax.ShapeDtypeStruct((4, high, width), jnp.bfloat16), TOKEN),
        scratch_shapes=[
            pltpu.VMEM((4, width, hidden_units), jnp.bfloat16),
            pltpu.VMEM((4, width, hidden_units), jnp.bfloat16),
            pltpu.VMEM((4, hidden_units, width), jnp.bfloat16),
            pltpu.VMEM((high, hidden_units), jnp.float32),
            pltpu.VMEM((high, hidden_units), jnp.float32),
            pltpu.VMEM((high, hidden_units), jnp.bfloat16),
            pltpu.SemaphoreType.DMA((3, 4)),
        ],
        compiler_params=pltpu.CompilerParams(vmem_limit_bytes=EXPERT_VMEM),
        cost_estimate=LIGHT,
    )(*operands)


def routed_experts(
    gained, squares, stats, expert_ids, expert_slots, slot_count, gate_w, up_w, down_w
):
    size = lax.axis_size("aa")
    index = lax.axis_index("aa")
    depth = lax.axis_size("ba")
    place = lax.axis_index("ba")
    over = functools.partial(lax.ppermute, axis_name="aa", perm=swap_pairs(size, 2))
    core = functools.partial(lax.ppermute, axis_name="aa", perm=swap_pairs(size, 1))

    def shift(array, by):
        return lax.ppermute(
            array, "ba", perm=[(at, (at + by) % depth) for at in range(depth)]
        )

    ahead = lax.rem(expert_ids - place + depth, depth)
    combined = ahead * slot_count + expert_slots
    chosen = (
        combined[:, None] == lax.broadcasted_iota(jnp.int32, (1, depth * slot_count), 1)
    ) & (expert_slots[:, None] >= 0)
    placing = chosen.astype(jnp.bfloat16)
    coarse = squares.astype(jnp.bfloat16)
    fine = (squares - coarse.astype(jnp.float32)).astype(jnp.bfloat16)
    rows = jnp.concatenate(
        [
            gained.astype(jnp.bfloat16),
            coarse,
            fine,
            jnp.zeros((gained.shape[0], HD - 2), jnp.bfloat16),
        ],
        axis=1,
    )
    slots = [slice(at * slot_count, (at + 1) * slot_count) for at in range(depth)]
    parts = [
        lax.dot_general(
            placing[:, slots[at]], rows, (((0,), (0,)), ((), ())), preferred_element_type=jnp.float32
        ).astype(jnp.bfloat16)
        for at in range(depth)
    ]

    def widen(block, far=None):
        far = over(block) if far is None else far
        both = core(jnp.stack([block, far]))
        return [block, far, both[0], both[1]]

    arrived = [parts[0], shift(parts[1], 1), None, shift(parts[3], 3)]
    arrived[2] = shift(parts[2], 2)
    quarter = jnp.stack([index, index ^ 2, index ^ 1, index ^ 3]).astype(jnp.int32)

    def narrow(share):
        return add(share[:2], core(share[2:]))

    weights = (gate_w, up_w, down_w)
    one, token = expert_call(quarter, [widen(arrived[0]), widen(arrived[1])], *weights)
    stats = after(stats.T, token)
    stats = stats + core(stats)
    stats = (stats + over(stats)).T
    one = narrow(one)
    low, high = slice(0, slot_count), slice(slot_count, 2 * slot_count)
    third = widen(arrived[3], after(over(arrived[3]), token))
    second = widen(after(arrived[2], token))
    two, token = expert_call(quarter, [third, second], *weights, stats)
    two = narrow(two)
    back = [None] * depth
    crossed = over(two[1, high])
    back[2] = shift(add(two[0, high], crossed), -2)
    back[3] = shift(add(two[0, low], over(two[1, low])), -3)
    near = over(after(one, crossed)[1, high])
    back[1] = shift(add(one[0, high], near), -1)
    back[0] = add(one[0, low], over(after(one, near)[1, low]))
    return lax.dot_general(
        placing,
        jnp.concatenate(back, axis=0),
        (((1,), (0,)), ((), ())),
        preferred_element_type=jnp.float32,
    ), stats


def gathered_experts(
    gained, squares, stats, expert_ids, expert_slots, slot_count, gate_w, up_w, down_w
):
    stats = lax.psum(stats, "aa")
    width = gained.shape[1] * lax.axis_size("aa")
    inverse = 1.0 / jnp.sqrt(stats[:, :1] / width + EPSILON)
    expert_in = (gained * inverse).astype(jnp.bfloat16)
    experts = gate_w.shape[0] * lax.axis_size("ba")
    combined = expert_ids * slot_count + expert_slots
    placing = (
        combined[:, None] == lax.broadcasted_iota(jnp.int32, (1, experts * slot_count), 1)
    ) & (expert_slots[:, None] >= 0)
    placing = placing.astype(jnp.bfloat16)
    packed = lax.dot_general(
        placing, expert_in, (((0,), (0,)), ((), ())), preferred_element_type=jnp.float32
    ).astype(jnp.bfloat16)
    arrived = lax.all_to_all(packed, "ba", split_axis=0, concat_axis=0, tiled=True)
    piece = lax.all_gather(arrived, "aa", axis=1, tiled=True)
    gate_part = jnp.dot(piece, gate_w[0], preferred_element_type=jnp.float32)
    up_part = jnp.dot(piece, up_w[0], preferred_element_type=jnp.float32)
    act = (jax.nn.silu(gate_part) * up_part).astype(jnp.bfloat16)
    expert_out = lax.psum_scatter(
        lax.dot_general(
            down_w[0], act, (((0,), (1,)), ((), ())), preferred_element_type=jnp.float32
        ).astype(jnp.bfloat16),
        "aa",
        scatter_dimension=0,
        tiled=True,
    )
    returned = lax.all_to_all(expert_out, "ba", split_axis=1, concat_axis=1, tiled=True)
    return lax.dot_general(
        placing, returned, (((1,), (1,)), ((), ())), preferred_element_type=jnp.float32
    ), stats


def on_device(
    query,
    keys,
    values,
    cache_lengths,
    residual,
    out_weight,
    norm_gain,
    router_weight,
    expert_ids,
    expert_slots,
    expert_gate,
    expert_up,
    expert_down,
):
    square = lax.axis_size("aa") == 4 and lax.axis_size("ba") == 4
    split = (
        square
        and keys.shape[1] == 2 * HD
        and keys.shape[0] % KEY_BLOCK == 0
        and query.shape[0] == residual.shape[0]
    )
    project = split_projection if split else plain_projection
    hidden = residual.astype(jnp.float32) + project(
        query, keys, values, cache_lengths, out_weight
    )
    width = hidden.shape[1] * lax.axis_size("aa")
    experts = router_weight.shape[1]
    gained = hidden * norm_gain
    squares = jnp.sum(hidden * hidden, axis=1, keepdims=True)
    raw = jnp.dot(gained, router_weight, precision=lax.Precision.HIGHEST)
    stats = jnp.concatenate([squares, raw], axis=1)

    slot_count = 2 * query.shape[0] * lax.axis_size("aa") // (lax.axis_size("ba") * experts)
    run = routed_experts if square and expert_gate.shape[0] == 1 else gathered_experts
    from_experts, sums = run(
        gained,
        squares,
        stats,
        expert_ids,
        expert_slots,
        slot_count,
        expert_gate,
        expert_up,
        expert_down,
    )
    logits = sums[:, 1:] / jnp.sqrt(sums[:, :1] / width + EPSILON)
    chosen = expert_ids[:, None] == lax.broadcasted_iota(jnp.int32, (1, experts), 1)
    gate = jnp.sum(jnp.where(chosen, jax.nn.sigmoid(logits), 0.0), axis=1)
    return (hidden + gate[:, None] * from_experts).astype(jnp.bfloat16)


def solution(mesh):
    return jax.shard_map(
        on_device,
        mesh=mesh,
        in_specs=(
            P(("ga", "aa"), "ba"),
            P(("ga", "aa"), "ba"),
            P(("ga", "aa"), "ba"),
            P(("ga", "aa")),
            P(("ga", "ba"), "aa"),
            P("ba", "aa"),
            P("aa"),
            P("aa", None),
            P(("ga", "ba")),
            P(("ga", "ba")),
            P("ba", None, "aa"),
            P("ba", None, "aa"),
            P("ba", "aa", None),
        ),
        out_specs=P(("ga", "ba"), "aa"),
        check_vma=False,
    )
```
